32 devices in a mesh: space: 4 (over y, x), blk: 8 (over z, core).
Axes of the slice: x: 2, y: 2, z: 4, core: 2. Of those that a mesh axis runs over, the one named last changes fastest.
Arguments:
- density: bfloat16 [3072, 128, 128], P(('space', 'blk')), may hold values from -6 to 6
- bra_table: bfloat16 [3072, 128, 256], P(('space', 'blk')), may hold values from -0.5 to 0.5
- ket_table: bfloat16 [3072, 128, 256], P(('space', 'blk')), may hold values from -0.5 to 0.5
- box_of_block: int32 [3072], P(('space', 'blk')), may hold values from 0 to 63
- leaf_src: int32 [256, 27], P(('space', 'blk')), may hold values from 0 to 191
- leaf_type: int32 [256, 27], P(('space', 'blk')), may hold values from 0 to 15
- coarse_src: int32 [32, 27], P(('space', 'blk')), may hold values from 0 to 31
- coarse_type: int32 [32, 27], P(('space', 'blk')), may hold values from 0 to 15
- translation: float32 [16, 256, 256], replicated, may hold values from -0.375 to 0.375
- upward_translation_table: float32 [8, 256, 256], replicated, may hold values from -0.375 to 0.375
Outputs:
- coulomb: bfloat16 [3072, 128, 128], P(('space', 'blk'))
- box_locals: float32 [256, 256], P(('space', 'blk'))
The draws below stay inside these ranges and needn't reach their ends.
All inputs are finite; a program needn't handle non-finite values.
Results may differ from the reference program's by a relative error of at most 0.0049.
Values sent between devices are 32-bit elements; how exact they have to be, the bound alone decides.
A program may use at most 128 MiB of HBM per device.

```python
import math
import jax
import jax.numpy as jnp
import numpy as np
from jax import lax

BS = 128
COEFF_COUNT = 256
BLK_DEV = 96
NLIST = 27
NCOARSE = 27
NTYPE = 16
BOX_DOM = 64
LEAF_BOX_COUNT = 256
PARENTS = 32
BLOCKS = 3072
N_SPACE = 4
N_BLK = 8


def place_ends(drawn, own_key, low, high):
    longest = drawn.shape.index(max(drawn.shape))
    spots = []
    for shift in (0, 1):
        where = [jax.random.randint(jax.random.fold_in(own_key, axis), (), 0, length) for axis, length in enumerate(drawn.shape)]
        where[longest] = (where[longest] + shift) % drawn.shape[longest]
        spots.append(tuple(where))
    return drawn.at[spots[0]].set(low).at[spots[1]].set(high)


def shard_levels(key, shape, shards, low, high):
    gain = 1.0
    for position, parts in shards:
        heights = jax.random.uniform(jax.random.fold_in(jax.random.fold_in(key, 6), position), (parts,), jnp.float32, low / len(shards), high / len(shards))
        gain = gain * jnp.repeat(jnp.exp(heights), shape[position] // parts).reshape((-1,) + (1,) * (len(shape) - 1 - position))
    return gain


def rank_table(number_of, slope):
    loads = [(1 << 20) // math.isqrt(rank ** slope) + 1 for rank in range(1, number_of + 1)]
    scale = 1 + sum(loads) // (1 << 30)
    return np.cumsum(np.array([max(1, weight // scale) for weight in loads]))


def ranked(rng, shape, count, slope):
    grid = rank_table(count, slope)
    pick = jax.random.randint(jax.random.fold_in(rng, 1), shape, 0, int(grid[count - 1]))
    grade = jnp.searchsorted(jnp.asarray(grid, jnp.int32), pick, side="right")
    return jax.random.permutation(jax.random.fold_in(rng, 2), count)[grade].astype(jnp.int32)


def gaussian(key, dims, deviation, most, pieces=(), held_as=jnp.bfloat16):
    loudness = shard_levels(key, dims, pieces, -0.22, 0.18) if pieces else 1.0
    entries = jax.random.normal(key, dims, jnp.float32) * deviation * loudness
    return jnp.minimum(jnp.maximum(entries, -most), most).astype(held_as)


def setup_inputs(seed: int = 0) -> dict:
    seeds = jax.random.split(jax.random.key(seed), 11)
    return {
        "density": gaussian(seeds[0], (BLOCKS, BS, BS), 1.0, 6.0, ((0, 32),)),
        "bra_table": gaussian(seeds[1], (BLOCKS, BS, COEFF_COUNT), BS ** -0.5, 0.5, ((0, 32),)),
        "ket_table": gaussian(seeds[2], (BLOCKS, BS, COEFF_COUNT), BS ** -0.5, 0.5, ((0, 32),)),
        "box_of_block": place_ends(ranked(seeds[3], (BLOCKS,), BOX_DOM, 2), jax.random.fold_in(seeds[3], 3), 0, BOX_DOM - 1).astype(jnp.int32),
        "leaf_src": place_ends(jax.random.randint(seeds[4], (LEAF_BOX_COUNT, NLIST), 0, 3 * BOX_DOM), jax.random.fold_in(seeds[4], 1), 0, (3 * BOX_DOM) - 1).astype(jnp.int32),
        "leaf_type": place_ends(jax.random.randint(seeds[5], (LEAF_BOX_COUNT, NLIST), 0, NTYPE), jax.random.fold_in(seeds[5], 1), 0, NTYPE - 1).astype(jnp.int32),
        "coarse_src": place_ends(jax.random.randint(seeds[6], (PARENTS, NCOARSE), 0, PARENTS), jax.random.fold_in(seeds[6], 1), 0, PARENTS - 1).astype(jnp.int32),
        "coarse_type": place_ends(jax.random.randint(seeds[7], (PARENTS, NCOARSE), 0, NTYPE), jax.random.fold_in(seeds[7], 1), 0, NTYPE - 1).astype(jnp.int32),
        "translation": gaussian(seeds[8], (NTYPE, COEFF_COUNT, COEFF_COUNT), COEFF_COUNT ** -0.5, 0.375, (), jnp.float32),
        "upward_translation_table": gaussian(seeds[9], (8, COEFF_COUNT, COEFF_COUNT), COEFF_COUNT ** -0.5, 0.375, (), jnp.float32),
    }


def block_group_moments(group):
    dens, bra, ket = group
    inner = jnp.einsum('bmn,bmk->bnk', dens.astype(jnp.float32), bra.astype(jnp.float32), precision=lax.Precision.HIGHEST)
    return jnp.sum(inner * ket.astype(jnp.float32), axis=1)


def reference(density, bra_table, ket_table, box_of_block, leaf_src, leaf_type, coarse_src, coarse_type, translation, upward_translation_table):
    top_level_index = lax.Precision.HIGHEST
    groups = N_SPACE * N_BLK
    dens_g = density.reshape(groups, BLK_DEV, BS, BS)
    bra_g = bra_table.reshape(groups, BLK_DEV, BS, COEFF_COUNT)
    ket_g = ket_table.reshape(groups, BLK_DEV, BS, COEFF_COUNT)
    moments = lax.map(block_group_moments, (dens_g, bra_g, ket_g)).reshape(N_SPACE, N_BLK * BLK_DEV, COEFF_COUNT)
    boxes = box_of_block.reshape(N_SPACE, N_BLK * BLK_DEV)
    box_hot = (boxes[:, :, None] == jnp.arange(BOX_DOM, dtype=jnp.int32)[None, None, :]).astype(jnp.float32)
    leaf_moments = jnp.einsum('sbj,sbk->sjk', box_hot, moments, precision=top_level_index)
    padded = jnp.concatenate([jnp.zeros((1, BOX_DOM, COEFF_COUNT), jnp.float32), leaf_moments, jnp.zeros((1, BOX_DOM, COEFF_COUNT), jnp.float32)], axis=0)
    windows = jnp.stack([padded[s:s + 3].reshape(3 * BOX_DOM, COEFF_COUNT) for s in range(N_SPACE)])
    src_hot = (leaf_src.reshape(N_SPACE, BOX_DOM, NLIST)[..., None] == jnp.arange(3 * BOX_DOM, dtype=jnp.int32)).astype(jnp.float32)
    type_hot = (leaf_type.reshape(N_SPACE, BOX_DOM, NLIST)[..., None] == jnp.arange(NTYPE, dtype=jnp.int32)).astype(jnp.float32)
    counts = jnp.einsum('sblt,sblj->sbtj', type_hot, src_hot, precision=top_level_index)
    gathered = jnp.einsum('sbtj,sjk->sbtk', counts, windows, precision=top_level_index)
    leaf_far = jnp.einsum('sbtk,tlk->sbl', gathered, translation, precision=top_level_index).reshape(LEAF_BOX_COUNT, COEFF_COUNT)
    child_boxes = leaf_moments.reshape(PARENTS, 8, COEFF_COUNT)
    parent_multipole_rows = jnp.einsum('ins,nrs->ir', child_boxes, upward_translation_table, precision=top_level_index)
    csrc_hot = (coarse_src[..., None] == jnp.arange(PARENTS, dtype=jnp.int32)).astype(jnp.float32)
    ctype_hot = (coarse_type[..., None] == jnp.arange(NTYPE, dtype=jnp.int32)).astype(jnp.float32)
    ccounts = jnp.einsum('pet,peq->ptq', ctype_hot, csrc_hot, precision=top_level_index)
    cgathered = jnp.einsum('ptq,qk->ptk', ccounts, parent_multipole_rows, precision=top_level_index)
    parent_local_rows = jnp.einsum('ptk,tlk->pl', cgathered, translation, precision=top_level_index)
    downward_sent = jnp.einsum('uh,nhq->unq', parent_local_rows, upward_translation_table, precision=top_level_index).reshape(LEAF_BOX_COUNT, COEFF_COUNT)
    box_locals = leaf_far + downward_sent
    dom_locals = box_locals.reshape(N_SPACE, BOX_DOM, COEFF_COUNT)
    block_locals = jnp.einsum('sbj,sjk->sbk', box_hot, dom_locals, precision=top_level_index).reshape(groups, BLK_DEV, COEFF_COUNT)

    def contract(group):
        bra, ket, local = group
        scaled = (bra.astype(jnp.float32) * local[:, None, :]).astype(jnp.bfloat16)
        return jnp.einsum('bmk,bnk->bmn', scaled.astype(jnp.float32), ket.astype(jnp.float32), precision=top_level_index).astype(jnp.bfloat16)

    coulomb = lax.map(contract, (bra_g, ket_g, block_locals)).reshape(BLOCKS, BS, BS)
    return coulomb, box_locals
```

```python
import functools

import jax
import jax.numpy as jnp
from jax import lax
from jax.experimental import pallas as pl
from jax.experimental.pallas import tpu as pltpu
from jax.sharding import PartitionSpec as P

MESH = pl.DeviceIdType.MESH
F32 = jnp.float32
BF16 = jnp.bfloat16
GROUP = 8
KEY = 1024


def dot(a, b, dims):
    return lax.dot_general(a, b, (dims, ((), ())), preferred_element_type=F32)


NN = ((1,), (0,))
NT = ((1,), (1,))
TN = ((0,), (0,))


def halves(x):
    high = x.astype(BF16)
    return high, (x - high.astype(F32)).astype(BF16)


def one_hot_dot(hot, x, dims):
    high, low = halves(x)
    return dot(hot, high, dims) + dot(hot, low, dims)


def split_dot(x, w, dims):
    rows = x.shape[0]
    x_high, x_low = halves(x)
    w_high, w_low = halves(w)
    both = dot(jnp.concatenate([x_high, x_low], axis=0), w_high, dims)
    return both[:rows] + both[rows:] + dot(x_high, w_low, dims)


def count_hot(keys, width):
    rows, entries = keys.shape
    lane = lax.broadcasted_iota(jnp.int32, (rows, width), 1)
    total = jnp.zeros((rows, width), F32)
    for e in range(entries):
        total += jnp.where(lane == keys[:, e : e + 1], 1.0, 0.0)
    return total


def build(
    n_space,
    n_blk,
    n_types,
    den_hbm, bra_hbm, ket_hbm, box_ref, lsrc_ref, ltype_ref, csrc_ref, ctype_ref, t_hbm, u_hbm,
    out_ref, mine_ref,
    den, bra, ket, t_ref, u_ref, mom, part, sib, lists, c_leaf, c_top, x_ref, v_high, v_low, v_top,
    leaf_out, top_out, leaf_in, top_in, dom, rows_ref, acc, kids,
    load_sem, table_sem, list_send, list_recv, sib_send, sib_recv,
    leaf_send, leaf_recv, top_send, top_recv, dom_send, dom_recv,
):
    s = lax.axis_index("space")
    j = lax.axis_index("blk")
    core = lax.rem(j, 2)
    z = j // 2
    other = j + 1 - 2 * core
    nz = n_blk // 2
    box_dom = 8 * n_blk
    top_dom = n_blk
    n_blocks = den.shape[0]
    chunks = n_blocks // GROUP
    entries = lsrc_ref.shape[1]
    me = s * nz + z
    groups = n_space * nz

    barrier = pltpu.get_barrier_semaphore()
    for o in range(1, groups):
        g = lax.rem(me + o, groups)
        pl.semaphore_signal(
            barrier, inc=1, device_id=(g // nz, lax.rem(g, nz) * 2 + core), device_id_type=MESH
        )
    for k in range(nz):
        pl.semaphore_signal(barrier, inc=1, device_id=(s, k * 2 + 1 - core), device_id_type=MESH)

    def loads(i):
        at = pl.ds(i * GROUP, GROUP)
        return [
            pltpu.make_async_copy(src.at[at], dst.at[at], load_sem.at[k, i])
            for k, (src, dst) in enumerate(((den_hbm, den), (ket_hbm, ket), (bra_hbm, bra)))
        ]

    def start_loads(i, carry):
        for copy in loads(i):
            copy.start()
        return carry

    lax.fori_loop(0, chunks, start_loads, 0)
    u_copy = pltpu.make_async_copy(u_hbm, u_ref, table_sem.at[0])
    t_copy = pltpu.make_async_copy(t_hbm, t_ref, table_sem.at[1])
    u_copy.start()
    t_copy.start()

    lists[pl.ds(me * 16, 8), 0:entries] = ltype_ref[...] * KEY + lsrc_ref[...]
    lists[pl.ds(me * 16 + 8, 1), 0:entries] = ctype_ref[...] * KEY + csrc_ref[...]
    pl.semaphore_wait(barrier, groups - 1 + nz)

    def list_copy(o):
        g = lax.rem(me + o, groups)
        at = pl.ds(me * 16, 16)
        return pltpu.make_async_remote_copy(
            src_ref=lists.at[at],
            dst_ref=lists.at[at],
            send_sem=list_send.at[o],
            recv_sem=list_recv.at[me],
            device_id=(g // nz, lax.rem(g, nz) * 2 + core),
            device_id_type=MESH,
        )

    def list_arrival(o):
        g = lax.rem(me + o, groups)
        at = pl.ds(g * 16, 16)
        return pltpu.make_async_remote_copy(
            src_ref=lists.at[at],
            dst_ref=lists.at[at],
            send_sem=list_send.at[o],
            recv_sem=list_recv.at[g],
            device_id=(g // nz, lax.rem(g, nz) * 2 + core),
            device_id_type=MESH,
        )

    for o in range(1, groups):
        list_copy(o).start()

    def moments(i, carry):
        for copy in loads(i):
            copy.wait()
        rows = []
        for u in range(GROUP):
            b = i * GROUP + u
            inner = dot(den[b], ket[b], NN)
            rows.append(jnp.sum(inner * bra[b].astype(F32), axis=0, keepdims=True))
        mom[pl.ds(i * GROUP, GROUP), :] = jnp.concatenate(rows, axis=0)
        return carry

    lax.fori_loop(0, chunks, moments, 0)
    hot = jnp.where(
        lax.broadcasted_iota(jnp.int32, (box_dom, n_blocks), 0) == box_ref[...], 1.0, 0.0
    ).astype(BF16)
    part[...] = one_hot_dot(hot, mom[...], NN)

    sib_copy = pltpu.make_async_remote_copy(
        src_ref=part,
        dst_ref=sib,
        send_sem=sib_send,
        recv_sem=sib_recv,
        device_id=(s, other),
        device_id_type=MESH,
    )
    sib_copy.start()

    for o in range(1, groups):
        list_arrival(o).wait_recv()
    for w in range(3):
        sender_at = 2 - w
        target = jnp.clip(s + w - 1, 0, n_space - 1)
        for k in range(nz):
            packed = lists[pl.ds((target * nz + k) * 16, 8), 0:entries]
            kind = lax.shift_right_logical(packed, 10)
            place = (packed & (KEY - 1)) - sender_at * box_dom
            keys = jnp.where((place >= 0) & (place < box_dom), kind * box_dom + place, -1)
            c_leaf[pl.ds((w * nz + k) * 8, 8), :] = count_hot(keys, n_types * box_dom)
    packed = lists[pl.ds(8, groups, stride=16), :]
    kind = lax.shift_right_logical(packed, 10)
    place = (packed & (KEY - 1)) - s * top_dom
    keys = jnp.where((place >= 0) & (place < top_dom), kind * top_dom + place, -1)
    c_top[...] = count_hot(keys[:, 0:entries], n_types * top_dom)

    u_copy.wait()
    t_copy.wait()
    sib_copy.wait()
    own = part[...] + sib[...]
    x_ref[0:box_dom, :] = own
    kids[0:box_dom, :] = own[:, 0:128]
    kids[box_dom:, :] = own[:, 128:]
    x_ref[box_dom:, :] = jnp.zeros((x_ref.shape[0] - box_dom, x_ref.shape[1]), F32)

    tops = jnp.zeros((top_dom, x_ref.shape[1]), F32)
    for c in range(8):
        child = jnp.concatenate(
            [kids[pl.ds(h * box_dom + c, top_dom, stride=8), :] for h in range(2)], axis=1
        )
        c_high, c_low = halves(child)
        stack = jnp.concatenate([c_high.astype(F32), c_low.astype(F32)], axis=0).astype(BF16)
        u_high, u_low = halves(u_ref[c])
        both = dot(stack, u_high, NT)
        extra = dot(stack, u_low, NT)
        tops += both[:top_dom] + both[top_dom:] + extra[:top_dom]
    x_ref[box_dom : box_dom + top_dom, :] = tops

    x = x_ref[...]
    x_high, x_low = halves(x)
    x_rows = x.shape[0]
    stack = jnp.concatenate([x_high, x_low], axis=0)
    for t in range(n_types):
        t_high, t_low = halves(t_ref[t])
        both = dot(stack, t_high, NT)
        v = both[:x_rows] + both[x_rows:] + dot(x_high, t_low, NT)
        high, low = halves(v[:box_dom])
        v_high[t * box_dom : (t + 1) * box_dom, :] = high
        v_low[t * box_dom : (t + 1) * box_dom, :] = low
        v_top[t * top_dom : (t + 1) * top_dom, :] = v[box_dom : box_dom + top_dom]

    sent_top = one_hot_dot(c_top[...].astype(BF16), v_top[...], NN)
    for g in range(groups):
        top_out[g] = sent_top[g : g + 1, :]

    def top_copy(o, source):
        g = lax.rem(me + o, groups)
        return pltpu.make_async_remote_copy(
            src_ref=top_out.at[g],
            dst_ref=top_in.at[source],
            send_sem=top_send.at[o],
            recv_sem=top_recv.at[source],
            device_id=(g // nz, lax.rem(g, nz) * 2 + core),
            device_id_type=MESH,
        )

    for o in range(1, groups):
        top_copy(o, me).start()
    top_in[pl.ds(me, 1)] = top_out[pl.ds(me, 1)]

    hot_leaf = c_leaf[...].astype(BF16)
    sent = dot(hot_leaf, v_high[...], NN) + dot(hot_leaf, v_low[...], NN)
    leaf_out[...] = sent.reshape(3 * nz, 8, sent.shape[1])

    def leaf_copy(w, o, source):
        k = lax.rem(z + o, nz)
        n = w * nz + o
        return pltpu.make_async_remote_copy(
            src_ref=leaf_out.at[w * nz + k],
            dst_ref=leaf_in.at[source],
            send_sem=leaf_send.at[n],
            recv_sem=leaf_recv.at[source],
            device_id=(jnp.clip(s + w - 1, 0, n_space - 1), k * 2 + core),
            device_id_type=MESH,
        )

    has = (s > 0, None, s < n_space - 1)
    for w in (0, 2):
        @pl.when(has[w])
        def _():
            for o in range(nz):
                leaf_copy(w, o, (2 - w) * nz + z).start()
    for o in range(1, nz):
        leaf_copy(1, o, nz + z).start()

    total = jnp.zeros((1, x_ref.shape[1]), F32)
    for o in range(1, groups):
        top_copy(o, lax.rem(me + o, groups)).wait_recv()
    for g in range(groups):
        total += top_in[g]
    total_high, total_low = halves(total)
    stack = jnp.concatenate(
        [total_high.astype(F32), total_low.astype(F32), jnp.zeros((14, total.shape[1]), F32)], axis=0
    ).astype(BF16)
    down = []
    for c in range(8):
        u_high, u_low = halves(u_ref[c])
        both = dot(stack, u_high, NN)
        extra = dot(stack, u_low, NN)
        down.append(both[0:1] + both[1:2] + extra[0:1])
    acc[...] = jnp.concatenate(down, axis=0) + leaf_out[pl.ds(nz + z, 1)][0]
    for o in range(1, nz):
        source = nz + lax.rem(z + o, nz)
        leaf_copy(1, o, source).wait_recv()
        acc[...] += leaf_in[pl.ds(source, 1)][0]
    for w in (0, 2):
        @pl.when(has[w])
        def _():
            for o in range(nz):
                source = w * nz + lax.rem(z + o, nz)
                leaf_copy(w, o, source).wait_recv()
                acc[...] += leaf_in[pl.ds(source, 1)][0]
    mine_ref[...] = acc[...]
    here = pl.ds(j * 8, 8)
    dom[here, :] = acc[...]

    def dom_copy(o, source):
        at = pl.ds(source * 8, 8)
        return pltpu.make_async_remote_copy(
            src_ref=dom.at[at],
            dst_ref=dom.at[at],
            send_sem=dom_send.at[o],
            recv_sem=dom_recv.at[source],
            device_id=(s, lax.rem(j + o, n_blk)),
            device_id_type=MESH,
        )

    for o in range(1, n_blk):
        dom_copy(o, j).start()
    for o in range(1, n_blk):
        dom_copy(o, lax.rem(j + o, n_blk)).wait_recv()

    rows_ref[...] = one_hot_dot(hot, dom[...], TN)

    def contract(i, carry):
        local = rows_ref[pl.ds(i * GROUP, GROUP), :]
        for u in range(GROUP):
            b = i * GROUP + u
            scaled = (bra[b].astype(F32) * local[u : u + 1, :]).astype(BF16)
            out_ref[b] = dot(scaled, ket[b], NT).astype(BF16)
        return carry

    lax.fori_loop(0, chunks, contract, 0)

    for o in range(1, groups):
        list_copy(o).wait_send()
        top_copy(o, me).wait_send()
    for w in (0, 2):
        @pl.when(has[w])
        def _():
            for o in range(nz):
                leaf_copy(w, o, (2 - w) * nz + z).wait_send()
    for o in range(1, nz):
        leaf_copy(1, o, nz + z).wait_send()
    for o in range(1, n_blk):
        dom_copy(o, j).wait_send()


def shards(
    density,
    bra_table,
    ket_table,
    box_of_block,
    leaf_src,
    leaf_type,
    coarse_src,
    coarse_type,
    translation,
    upward_translation_table,
):
    n_space = lax.axis_size("space")
    n_blk = lax.axis_size("blk")
    nz = n_blk // 2
    groups = n_space * nz
    n_blocks, side, coeffs = bra_table.shape
    n_types = translation.shape[0]
    box_dom = 8 * n_blk
    top_dom = n_blk
    chunks = n_blocks // GROUP
    x_rows = -(-(box_dom + top_dom) // 16) * 16
    whole = pl.BlockSpec(memory_space=pltpu.VMEM)
    far = pl.BlockSpec(memory_space=pl.ANY)
    dma = pltpu.SemaphoreType.DMA
    coulomb, box_locals = pl.pallas_call(
        functools.partial(build, n_space, n_blk, n_types),
        out_shape=(
            jax.ShapeDtypeStruct((n_blocks, side, side), BF16),
            jax.ShapeDtypeStruct((8, coeffs), F32),
        ),
        in_specs=[far, far, far, whole, whole, whole, whole, whole, far, far],
        out_specs=(whole, whole),
        scratch_shapes=[
            pltpu.VMEM(density.shape, BF16),
            pltpu.VMEM(bra_table.shape, BF16),
            pltpu.VMEM(ket_table.shape, BF16),
            pltpu.VMEM(translation.shape, F32),
            pltpu.VMEM(upward_translation_table.shape, F32),
            pltpu.VMEM((n_blocks, coeffs), F32),
            pltpu.VMEM((box_dom, coeffs), F32),
            pltpu.VMEM((box_dom, coeffs), F32),
            pltpu.VMEM((groups * 16, 128), jnp.int32),
            pltpu.VMEM((3 * nz * 8, n_types * box_dom), F32),
            pltpu.VMEM((groups, n_types * top_dom), F32),
            pltpu.VMEM((x_rows, coeffs), F32),
            pltpu.VMEM((n_types * box_dom, coeffs), BF16),
            pltpu.VMEM((n_types * box_dom, coeffs), BF16),
            pltpu.VMEM((n_types * top_dom, coeffs), F32),
            pltpu.VMEM((3 * nz, 8, coeffs), F32),
            pltpu.VMEM((groups, 1, coeffs), F32),
            pltpu.VMEM((3 * nz, 8, coeffs), F32),
            pltpu.VMEM((groups, 1, coeffs), F32),
            pltpu.VMEM((box_dom, coeffs), F32),
            pltpu.VMEM((n_blocks, coeffs), F32),
            pltpu.VMEM((8, coeffs), F32),
            pltpu.VMEM((2 * box_dom, coeffs // 2), F32),
            dma((3, chunks)),
            dma((2,)),
            dma((groups,)),
            dma((groups,)),
            dma,
            dma,
            dma((3 * nz,)),
            dma((3 * nz,)),
            dma((groups,)),
            dma((groups,)),
            dma((n_blk,)),
            dma((n_blk,)),
        ],
        compiler_params=pltpu.CompilerParams(
            collective_id=0, has_side_effects=True, vmem_limit_bytes=48 * 1024 * 1024
        ),
        cost_estimate=pl.CostEstimate(
            flops=4 * n_blocks * side * side * coeffs,
            bytes_accessed=30_000_000,
            transcendentals=0,
        ),
    )(
        density,
        bra_table,
        ket_table,
        box_of_block[None, :],
        leaf_src,
        leaf_type,
        coarse_src,
        coarse_type,
        translation,
        upward_translation_table,
    )
    return coulomb, box_locals


def solution(mesh):
    placed = (
        P(("space", "blk"), None, None),
        P(("space", "blk"), None, None),
        P(("space", "blk"), None, None),
        P(("space", "blk")),
        P(("space", "blk"), None),
        P(("space", "blk"), None),
        P(("space", "blk"), None),
        P(("space", "blk"), None),
        P(),
        P(),
    )
    return jax.shard_map(
        shards,
        mesh=mesh,
        in_specs=placed,
        out_specs=(P(("space", "blk"), None, None), P(("space", "blk"), None)),
        check_vma=False,
    )
```

```python
import functools

import jax
import jax.numpy as jnp
from jax import lax
from jax.experimental import pallas as pl
from jax.experimental.pallas import tpu as pltpu
from jax.sharding import PartitionSpec as P

MESH = pl.DeviceIdType.MESH
F32 = jnp.float32
BF16 = jnp.bfloat16
GROUP = 8
KEY = 1024


def dot(a, b, dims):
    return lax.dot_general(a, b, (dims, ((), ())), preferred_element_type=F32)


NN = ((1,), (0,))
NT = ((1,), (1,))
TN = ((0,), (0,))


def halves(x):
    high = x.astype(BF16)
    return high, (x - high.astype(F32)).astype(BF16)


def one_hot_dot(hot, x, dims):
    high, low = halves(x)
    return dot(hot, high, dims) + dot(hot, low, dims)


def count_hot(keys, width):
    rows, entries = keys.shape
    lane = lax.broadcasted_iota(jnp.int32, (rows, width), 1)
    total = jnp.zeros((rows, width), F32)
    for e in range(entries):
        total += jnp.where(lane == keys[:, e : e + 1], 1.0, 0.0)
    return total


def build(
    n_space,
    n_blk,
    n_types,
    den_hbm, bra_hbm, ket_hbm, box_hbm, lsrc_hbm, ltype_hbm, csrc_hbm, ctype_hbm, t_hbm, u_hbm,
    bra, ket, rows_ref, mine_ref,
    box_ref, lsrc_ref, ltype_ref, csrc_ref, ctype_ref, den, t_ref, u_ref, mom, part, sib, lists, c_leaf, c_top, x_ref, v_high, v_low, v_top,
    leaf_out, top_out, leaf_in, top_in, dom, acc, kids,
    small_sem, load_sem, table_sem, list_send, list_recv, sib_send, sib_recv,
    leaf_send, leaf_recv, top_send, top_recv, dom_send, dom_recv,
):
    s = lax.axis_index("space")
    j = lax.axis_index("blk")
    core = lax.rem(j, 2)
    z = j // 2
    other = j + 1 - 2 * core
    nz = n_blk // 2
    box_dom = 8 * n_blk
    top_dom = n_blk
    n_blocks = den.shape[0]
    chunks = n_blocks // GROUP
    entries = lsrc_ref.shape[1]
    me = s * nz + z
    groups = n_space * nz

    small = [
        pltpu.make_async_copy(src, dst, small_sem.at[k])
        for k, (src, dst) in enumerate(
            (
                (ltype_hbm, ltype_ref),
                (lsrc_hbm, lsrc_ref),
                (ctype_hbm, ctype_ref),
                (csrc_hbm, csrc_ref),
                (box_hbm, box_ref),
            )
        )
    ]

    def loads(i):
        at = pl.ds(i * GROUP, GROUP)
        return [
            pltpu.make_async_copy(src.at[at], dst.at[at], load_sem.at[k, i])
            for k, (src, dst) in enumerate(((den_hbm, den), (ket_hbm, ket), (bra_hbm, bra)))
        ]

    def start_loads(i, carry):
        for copy in loads(i):
            copy.start()
        return carry

    start_loads(0, 0)
    for copy in small:
        copy.start()

    barrier = pltpu.get_barrier_semaphore()
    for o in range(1, groups):
        g = lax.rem(me + o, groups)
        pl.semaphore_signal(
            barrier, inc=1, device_id=(g // nz, lax.rem(g, nz) * 2 + core), device_id_type=MESH
        )
    for k in range(nz):
        pl.semaphore_signal(barrier, inc=1, device_id=(s, k * 2 + 1 - core), device_id_type=MESH)

    lax.fori_loop(1, chunks, start_loads, 0)
    u_copy = pltpu.make_async_copy(u_hbm, u_ref, table_sem.at[0])
    t_copy = pltpu.make_async_copy(t_hbm, t_ref, table_sem.at[1])
    u_copy.start()
    t_copy.start()

    def moments(i, carry):
        for copy in loads(i):
            copy.wait()
        rows = []
        for u in range(GROUP):
            b = i * GROUP + u
            inner = dot(den[b], ket[b], NN)
            rows.append(jnp.sum(inner * bra[b].astype(F32), axis=0, keepdims=True))
        mom[pl.ds(i * GROUP, GROUP), :] = jnp.concatenate(rows, axis=0)
        return carry

    lax.fori_loop(0, chunks // 2, moments, 0)

    for copy in small:
        copy.wait()
    lists[pl.ds(me * 16, 8), 0:entries] = ltype_ref[...] * KEY + lsrc_ref[...]
    lists[pl.ds(me * 16 + 8, 1), 0:entries] = ctype_ref[...] * KEY + csrc_ref[...]
    pl.semaphore_wait(barrier, groups - 1 + nz)

    def list_copy(o):
        g = lax.rem(me + o, groups)
        at = pl.ds(me * 16, 16)
        return pltpu.make_async_remote_copy(
            src_ref=lists.at[at],
            dst_ref=lists.at[at],
            send_sem=list_send.at[o],
            recv_sem=list_recv.at[me],
            device_id=(g // nz, lax.rem(g, nz) * 2 + core),
            device_id_type=MESH,
        )

    def list_arrival(o):
        g = lax.rem(me + o, groups)
        at = pl.ds(g * 16, 16)
        return pltpu.make_async_remote_copy(
            src_ref=lists.at[at],
            dst_ref=lists.at[at],
            send_sem=list_send.at[o],
            recv_sem=list_recv.at[g],
            device_id=(g // nz, lax.rem(g, nz) * 2 + core),
            device_id_type=MESH,
        )

    for o in range(1, groups):
        list_copy(o).start()

    lax.fori_loop(chunks // 2, chunks, moments, 0)
    hot = jnp.where(
        lax.broadcasted_iota(jnp.int32, (box_dom, n_blocks), 0) == box_ref[...], 1.0, 0.0
    ).astype(BF16)
    part[...] = one_hot_dot(hot, mom[...], NN)

    sib_copy = pltpu.make_async_remote_copy(
        src_ref=part,
        dst_ref=sib,
        send_sem=sib_send,
        recv_sem=sib_recv,
        device_id=(s, other),
        device_id_type=MESH,
    )
    sib_copy.start()

    for o in range(1, groups):
        list_arrival(o).wait_recv()
    for w in range(3):
        sender_at = 2 - w
        target = jnp.clip(s + w - 1, 0, n_space - 1)
        for k in range(nz):
            packed = lists[pl.ds((target * nz + k) * 16, 8), 0:entries]
            kind = lax.shift_right_logical(packed, 10)
            place = (packed & (KEY - 1)) - sender_at * box_dom
            keys = jnp.where((place >= 0) & (place < box_dom), kind * box_dom + place, -1)
            c_leaf[pl.ds((w * nz + k) * 8, 8), :] = count_hot(keys, n_types * box_dom)
    packed = lists[pl.ds(8, groups, stride=16), :]
    kind = lax.shift_right_logical(packed, 10)
    place = (packed & (KEY - 1)) - s * top_dom
    keys = jnp.where((place >= 0) & (place < top_dom), kind * top_dom + place, -1)
    c_top[...] = count_hot(keys[:, 0:entries], n_types * top_dom)

    u_copy.wait()
    t_copy.wait()
    sib_copy.wait()
    own = part[...] + sib[...]
    x_ref[0:box_dom, :] = own
    kids[0:box_dom, :] = own[:, 0:128]
    kids[box_dom:, :] = own[:, 128:]
    x_ref[box_dom:, :] = jnp.zeros((x_ref.shape[0] - box_dom, x_ref.shape[1]), F32)

    tops = jnp.zeros((top_dom, x_ref.shape[1]), F32)
    for c in range(8):
        child = jnp.concatenate(
            [kids[pl.ds(h * box_dom + c, top_dom, stride=8), :] for h in range(2)], axis=1
        )
        c_high, c_low = halves(child)
        stack = jnp.concatenate([c_high.astype(F32), c_low.astype(F32)], axis=0).astype(BF16)
        u_high, u_low = halves(u_ref[c])
        both = dot(stack, u_high, NT)
        extra = dot(stack, u_low, NT)
        tops += both[:top_dom] + both[top_dom:] + extra[:top_dom]
    x_ref[box_dom : box_dom + top_dom, :] = tops

    x = x_ref[...]
    x_high, x_low = halves(x)
    x_rows = x.shape[0]
    stack = jnp.concatenate([x_high, x_low], axis=0)
    for t in range(n_types):
        t_high, t_low = halves(t_ref[t])
        both = dot(stack, t_high, NT)
        v = both[:x_rows] + both[x_rows:] + dot(x_high, t_low, NT)
        high, low = halves(v[:box_dom])
        v_high[t * box_dom : (t + 1) * box_dom, :] = high
        v_low[t * box_dom : (t + 1) * box_dom, :] = low
        v_top[t * top_dom : (t + 1) * top_dom, :] = v[box_dom : box_dom + top_dom]

    sent_top = one_hot_dot(c_top[...].astype(BF16), v_top[...], NN)
    for g in range(groups):
        top_out[g] = sent_top[g : g + 1, :]

    def top_copy(o, source):
        g = lax.rem(me + o, groups)
        return pltpu.make_async_remote_copy(
            src_ref=top_out.at[g],
            dst_ref=top_in.at[source],
            send_sem=top_send.at[o],
            recv_sem=top_recv.at[source],
            device_id=(g // nz, lax.rem(g, nz) * 2 + core),
            device_id_type=MESH,
        )

    for o in range(1, groups):
        top_copy(o, me).start()
    top_in[pl.ds(me, 1)] = top_out[pl.ds(me, 1)]

    hot_leaf = c_leaf[...].astype(BF16)
    sent = dot(hot_leaf, v_high[...], NN) + dot(hot_leaf, v_low[...], NN)
    leaf_out[...] = sent.reshape(3 * nz, 8, sent.shape[1])

    def leaf_copy(w, o, source):
        k = lax.rem(z + o, nz)
        n = w * nz + o
        return pltpu.make_async_remote_copy(
            src_ref=leaf_out.at[w * nz + k],
            dst_ref=leaf_in.at[source],
            send_sem=leaf_send.at[n],
            recv_sem=leaf_recv.at[source],
            device_id=(jnp.clip(s + w - 1, 0, n_space - 1), k * 2 + core),
            device_id_type=MESH,
        )

    has = (s > 0, None, s < n_space - 1)
    for w in (0, 2):
        @pl.when(has[w])
        def _():
            for o in range(nz):
                leaf_copy(w, o, (2 - w) * nz + z).start()
    for o in range(1, nz):
        leaf_copy(1, o, nz + z).start()

    total = jnp.zeros((1, x_ref.shape[1]), F32)
    for o in range(1, groups):
        top_copy(o, lax.rem(me + o, groups)).wait_recv()
    for g in range(groups):
        total += top_in[g]
    total_high, total_low = halves(total)
    stack = jnp.concatenate(
        [total_high.astype(F32), total_low.astype(F32), jnp.zeros((14, total.shape[1]), F32)], axis=0
    ).astype(BF16)
    down = []
    for c in range(8):
        u_high, u_low = halves(u_ref[c])
        both = dot(stack, u_high, NN)
        extra = dot(stack, u_low, NN)
        down.append(both[0:1] + both[1:2] + extra[0:1])
    acc[...] = jnp.concatenate(down, axis=0) + leaf_out[pl.ds(nz + z, 1)][0]
    for o in range(1, nz):
        source = nz + lax.rem(z + o, nz)
        leaf_copy(1, o, source).wait_recv()
        acc[...] += leaf_in[pl.ds(source, 1)][0]
    for w in (0, 2):
        @pl.when(has[w])
        def _():
            for o in range(nz):
                source = w * nz + lax.rem(z + o, nz)
                leaf_copy(w, o, source).wait_recv()
                acc[...] += leaf_in[pl.ds(source, 1)][0]
    mine_ref[...] = acc[...]
    here = pl.ds(j * 8, 8)
    dom[here, :] = acc[...]

    def dom_copy(o, source):
        at = pl.ds(source * 8, 8)
        return pltpu.make_async_remote_copy(
            src_ref=dom.at[at],
            dst_ref=dom.at[at],
            send_sem=dom_send.at[o],
            recv_sem=dom_recv.at[source],
            device_id=(s, lax.rem(j + o, n_blk)),
            device_id_type=MESH,
        )

    for o in range(1, n_blk):
        dom_copy(o, j).start()

    for o in range(1, groups):
        list_copy(o).wait_send()
        top_copy(o, me).wait_send()
    for w in (0, 2):
        @pl.when(has[w])
        def _():
            for o in range(nz):
                leaf_copy(w, o, (2 - w) * nz + z).wait_send()
    for o in range(1, nz):
        leaf_copy(1, o, nz + z).wait_send()

    for o in range(1, n_blk):
        dom_copy(o, lax.rem(j + o, n_blk)).wait_recv()
    rows_ref[...] = one_hot_dot(hot, dom[...], TN)
    for o in range(1, n_blk):
        dom_copy(o, j).wait_send()


def contract(bra, ket, rows_ref, mine_ref, out_hbm, mine_hbm, out, out_sem, mine_sem):
    chunks = bra.shape[0] // GROUP
    mine_copy = pltpu.make_async_copy(mine_ref, mine_hbm, mine_sem)
    mine_copy.start()

    def store(i):
        at = pl.ds(i * GROUP, GROUP)
        return pltpu.make_async_copy(out.at[at], out_hbm.at[at], out_sem.at[i])

    def step(i, carry):
        local = rows_ref[pl.ds(i * GROUP, GROUP), :]
        for u in range(GROUP):
            b = i * GROUP + u
            scaled = (bra[b].astype(F32) * local[u : u + 1, :]).astype(BF16)
            out[b] = dot(scaled, ket[b], NT).astype(BF16)
        store(i).start()
        return carry

    lax.fori_loop(0, chunks, step, 0)
    for i in range(chunks):
        store(i).wait()
    mine_copy.wait()


def shards(
    density,
    bra_table,
    ket_table,
    box_of_block,
    leaf_src,
    leaf_type,
    coarse_src,
    coarse_type,
    translation,
    upward_translation_table,
):
    n_space = lax.axis_size("space")
    n_blk = lax.axis_size("blk")
    nz = n_blk // 2
    groups = n_space * nz
    n_blocks, side, coeffs = bra_table.shape
    n_types = translation.shape[0]
    box_dom = 8 * n_blk
    top_dom = n_blk
    chunks = n_blocks // GROUP
    x_rows = -(-(box_dom + top_dom) // 16) * 16
    whole = pl.BlockSpec(memory_space=pltpu.VMEM)
    far = pl.BlockSpec(memory_space=pltpu.HBM)
    dma = pltpu.SemaphoreType.DMA
    ints = jnp.int32
    bra_here, ket_here, rows, mine = pl.pallas_call(
        functools.partial(build, n_space, n_blk, n_types),
        out_shape=(
            jax.ShapeDtypeStruct(bra_table.shape, BF16),
            jax.ShapeDtypeStruct(ket_table.shape, BF16),
            jax.ShapeDtypeStruct((n_blocks, coeffs), F32),
            jax.ShapeDtypeStruct((8, coeffs), F32),
        ),
        in_specs=[far] * 10,
        out_specs=(whole,) * 4,
        scratch_shapes=[
            pltpu.VMEM((1, n_blocks), ints),
            pltpu.VMEM(leaf_src.shape, ints),
            pltpu.VMEM(leaf_type.shape, ints),
            pltpu.VMEM(coarse_src.shape, ints),
            pltpu.VMEM(coarse_type.shape, ints),
            pltpu.VMEM(density.shape, BF16),
            pltpu.VMEM(translation.shape, F32),
            pltpu.VMEM(upward_translation_table.shape, F32),
            pltpu.VMEM((n_blocks, coeffs), F32),
            pltpu.VMEM((box_dom, coeffs), F32),
            pltpu.VMEM((box_dom, coeffs), F32),
            pltpu.VMEM((groups * 16, 128), jnp.int32),
            pltpu.VMEM((3 * nz * 8, n_types * box_dom), F32),
            pltpu.VMEM((groups, n_types * top_dom), F32),
            pltpu.VMEM((x_rows, coeffs), F32),
            pltpu.VMEM((n_types * box_dom, coeffs), BF16),
            pltpu.VMEM((n_types * box_dom, coeffs), BF16),
            pltpu.VMEM((n_types * top_dom, coeffs), F32),
            pltpu.VMEM((3 * nz, 8, coeffs), F32),
            pltpu.VMEM((groups, 1, coeffs), F32),
            pltpu.VMEM((3 * nz, 8, coeffs), F32),
            pltpu.VMEM((groups, 1, coeffs), F32),
            pltpu.VMEM((box_dom, coeffs), F32),
            pltpu.VMEM((8, coeffs), F32),
            pltpu.VMEM((2 * box_dom, coeffs // 2), F32),
            dma((5,)),
            dma((3, chunks)),
            dma((2,)),
            dma((groups,)),
            dma((groups,)),
            dma,
            dma,
            dma((3 * nz,)),
            dma((3 * nz,)),
            dma((groups,)),
            dma((groups,)),
            dma((n_blk,)),
            dma((n_blk,)),
        ],
        compiler_params=pltpu.CompilerParams(
            collective_id=0, has_side_effects=True, vmem_limit_bytes=28 * 1024 * 1024
        ),
        cost_estimate=pl.CostEstimate(
            flops=2 * n_blocks * side * side * coeffs,
            bytes_accessed=22_000_000,
            transcendentals=0,
        ),
    )(
        *(
            pltpu.with_memory_space_constraint(x, pltpu.HBM)
            for x in (
                density,
                bra_table,
                ket_table,
                box_of_block[None, :],
                leaf_src,
                leaf_type,
                coarse_src,
                coarse_type,
                translation,
                upward_translation_table,
            )
        )
    )
    return pl.pallas_call(
        contract,
        out_shape=(
            jax.ShapeDtypeStruct((n_blocks, side, side), BF16),
            jax.ShapeDtypeStruct((8, coeffs), F32),
        ),
        in_specs=[whole] * 4,
        out_specs=(far, far),
        scratch_shapes=[
            pltpu.VMEM((n_blocks, side, side), BF16),
            dma((chunks,)),
            dma,
        ],
        compiler_params=pltpu.CompilerParams(vmem_limit_bytes=16 * 1024 * 1024),
        cost_estimate=pl.CostEstimate(
            flops=2 * n_blocks * side * side * coeffs,
            bytes_accessed=2 * n_blocks * side * side,
            transcendentals=0,
        ),
    )(bra_here, ket_here, rows, mine)


def solution(mesh):
    placed = (
        P(("space", "blk"), None, None),
        P(("space", "blk"), None, None),
        P(("space", "blk"), None, None),
        P(("space", "blk")),
        P(("space", "blk"), None),
        P(("space", "blk"), None),
        P(("space", "blk"), None),
        P(("space", "blk"), None),
        P(),
        P(),
    )
    return jax.shard_map(
        shards,
        mesh=mesh,
        in_specs=placed,
        out_specs=(P(("space", "blk"), None, None), P(("space", "blk"), None)),
        check_vma=False,
    )
```

```python
import functools

import jax
import jax.numpy as jnp
from jax import lax
from jax.experimental import pallas as pl
from jax.experimental.pallas import tpu as pltpu
from jax.sharding import PartitionSpec as P

MESH = pl.DeviceIdType.MESH
F32 = jnp.float32
BF16 = jnp.bfloat16
GROUP = 16
UNROLL = 4
KEY = 1024


def dot(a, b, dims):
    return lax.dot_general(a, b, (dims, ((), ())), preferred_element_type=F32)


NN = ((1,), (0,))
NT = ((1,), (1,))
TN = ((0,), (0,))


def halves(x):
    high = x.astype(BF16)
    return high, (x - high.astype(F32)).astype(BF16)


def one_hot_dot(hot, x, dims):
    high, low = halves(x)
    return dot(hot, high, dims) + dot(hot, low, dims)


def count_hot(keys, width):
    rows, entries = keys.shape
    lane = lax.broadcasted_iota(jnp.int32, (rows, width), 1)
    total = jnp.zeros((rows, width), F32)
    for e in range(entries):
        total += jnp.where(lane == keys[:, e : e + 1], 1.0, 0.0)
    return total


def build(
    n_space,
    n_blk,
    n_types,
    den_hbm, bra_hbm, ket_hbm, box_hbm, lsrc_hbm, ltype_hbm, csrc_hbm, ctype_hbm, t_hbm, u_hbm,
    bra, ket, rows_ref, mine_ref,
    box_ref, lsrc_ref, ltype_ref, csrc_ref, ctype_ref, den, t_ref, u_ref, mom, part, sib, lists, c_leaf, c_top, x_ref, v_high, v_low, v_top,
    leaf_out, top_out, leaf_in, top_in, dom, acc, kids,
    small_sem, load_sem, table_sem, list_send, list_recv, sib_send, sib_recv,
    leaf_send, leaf_recv, top_send, top_recv, dom_send, dom_recv,
):
    s = lax.axis_index("space")
    j = lax.axis_index("blk")
    core = lax.rem(j, 2)
    z = j // 2
    other = j + 1 - 2 * core
    nz = n_blk // 2
    box_dom = 8 * n_blk
    top_dom = n_blk
    n_blocks = den.shape[0]
    chunks = n_blocks // GROUP
    entries = lsrc_ref.shape[1]
    me = s * nz + z
    groups = n_space * nz

    small = [
        pltpu.make_async_copy(src, dst, small_sem.at[k])
        for k, (src, dst) in enumerate(
            (
                (ltype_hbm, ltype_ref),
                (lsrc_hbm, lsrc_ref),
                (ctype_hbm, ctype_ref),
                (csrc_hbm, csrc_ref),
                (box_hbm, box_ref),
            )
        )
    ]

    def loads(i):
        at = pl.ds(i * GROUP, GROUP)
        return [
            pltpu.make_async_copy(src.at[at], dst.at[at], load_sem.at[k, i])
            for k, (src, dst) in enumerate(((den_hbm, den), (ket_hbm, ket), (bra_hbm, bra)))
        ]

    def start_loads(i, carry):
        for copy in loads(i):
            copy.start()
        return carry

    start_loads(0, 0)
    for copy in small:
        copy.start()

    barrier = pltpu.get_barrier_semaphore()
    for o in range(1, groups):
        g = lax.rem(me + o, groups)
        pl.semaphore_signal(
            barrier, inc=1, device_id=(g // nz, lax.rem(g, nz) * 2 + core), device_id_type=MESH
        )
    for k in range(nz):
        pl.semaphore_signal(barrier, inc=1, device_id=(s, k * 2 + 1 - core), device_id_type=MESH)

    lax.fori_loop(1, chunks, start_loads, 0)
    u_copy = pltpu.make_async_copy(u_hbm, u_ref, table_sem.at[0])
    t_copy = pltpu.make_async_copy(t_hbm, t_ref, table_sem.at[1])

    def moments(i, carry):
        for copy in loads(i):
            copy.wait()
        rows = []
        for u in range(GROUP):
            b = i * GROUP + u
            inner = dot(den[b], ket[b], NN)
            rows.append(jnp.sum(inner * bra[b].astype(F32), axis=0, keepdims=True))
        mom[pl.ds(i * GROUP, GROUP), :] = jnp.concatenate(rows, axis=0)
        return carry

    lax.fori_loop(0, chunks // 2, moments, 0)
    u_copy.start()
    t_copy.start()

    for copy in small:
        copy.wait()
    lists[pl.ds(me * 16, 8), 0:entries] = ltype_ref[...] * KEY + lsrc_ref[...]
    lists[pl.ds(me * 16 + 8, 1), 0:entries] = ctype_ref[...] * KEY + csrc_ref[...]
    pl.semaphore_wait(barrier, groups - 1 + nz)

    def list_copy(o):
        g = lax.rem(me + o, groups)
        at = pl.ds(me * 16, 16)
        return pltpu.make_async_remote_copy(
            src_ref=lists.at[at],
            dst_ref=lists.at[at],
            send_sem=list_send.at[o],
            recv_sem=list_recv.at[me],
            device_id=(g // nz, lax.rem(g, nz) * 2 + core),
            device_id_type=MESH,
        )

    def list_arrival(o):
        g = lax.rem(me + o, groups)
        at = pl.ds(g * 16, 16)
        return pltpu.make_async_remote_copy(
            src_ref=lists.at[at],
            dst_ref=lists.at[at],
            send_sem=list_send.at[o],
            recv_sem=list_recv.at[g],
            device_id=(g // nz, lax.rem(g, nz) * 2 + core),
            device_id_type=MESH,
        )

    for o in range(1, groups):
        list_copy(o).start()

    lax.fori_loop(chunks // 2, chunks, moments, 0)
    hot = jnp.where(
        lax.broadcasted_iota(jnp.int32, (box_dom, n_blocks), 0) == box_ref[...], 1.0, 0.0
    ).astype(BF16)
    part[...] = one_hot_dot(hot, mom[...], NN)

    sib_copy = pltpu.make_async_remote_copy(
        src_ref=part,
        dst_ref=sib,
        send_sem=sib_send,
        recv_sem=sib_recv,
        device_id=(s, other),
        device_id_type=MESH,
    )
    sib_copy.start()

    for o in range(1, groups):
        list_arrival(o).wait_recv()
    def counts(n, carry):
        w = n // nz
        target = jnp.clip(s + w - 1, 0, n_space - 1) * nz + lax.rem(n, nz)
        packed = lists[pl.ds(pl.multiple_of(target * 16, 16), 8), 0:entries]
        kind = lax.shift_right_logical(packed, 10)
        place = (packed & (KEY - 1)) - (2 - w) * box_dom
        keys = jnp.where((place >= 0) & (place < box_dom), kind * box_dom + place, -1)
        c_leaf[pl.ds(pl.multiple_of(n * 8, 8), 8), :] = count_hot(keys, n_types * box_dom)
        return carry

    lax.fori_loop(0, 3 * nz, counts, 0)
    packed = lists[pl.ds(8, groups, stride=16), :]
    kind = lax.shift_right_logical(packed, 10)
    place = (packed & (KEY - 1)) - s * top_dom
    keys = jnp.where((place >= 0) & (place < top_dom), kind * top_dom + place, -1)
    c_top[...] = count_hot(keys[:, 0:entries], n_types * top_dom)

    u_copy.wait()
    t_copy.wait()
    sib_copy.wait()
    own = part[...] + sib[...]
    x_ref[0:box_dom, :] = own
    kids[0:box_dom, :] = own[:, 0:128]
    kids[box_dom:, :] = own[:, 128:]
    x_ref[box_dom:, :] = jnp.zeros((x_ref.shape[0] - box_dom, x_ref.shape[1]), F32)

    tops = jnp.zeros((top_dom, x_ref.shape[1]), F32)
    for c in range(8):
        child = jnp.concatenate(
            [kids[pl.ds(h * box_dom + c, top_dom, stride=8), :] for h in range(2)], axis=1
        )
        c_high, c_low = halves(child)
        stack = jnp.concatenate([c_high.astype(F32), c_low.astype(F32)], axis=0).astype(BF16)
        u_high, u_low = halves(u_ref[c])
        both = dot(stack, u_high, NT)
        extra = dot(stack, u_low, NT)
        tops += both[:top_dom] + both[top_dom:] + extra[:top_dom]
    x_ref[box_dom : box_dom + top_dom, :] = tops

    x = x_ref[...]
    x_high, x_low = halves(x)
    x_rows = x.shape[0]
    stack = jnp.concatenate([x_high, x_low], axis=0)
    def translate(i, carry):
        for u in range(UNROLL):
            t = i * UNROLL + u
            t_high, t_low = halves(t_ref[t])
            both = dot(stack, t_high, NT)
            v = both[:x_rows] + both[x_rows:] + dot(x_high, t_low, NT)
            high, low = halves(v[:box_dom])
            at = pl.ds(pl.multiple_of(t * box_dom, 16), box_dom)
            v_high[at, :] = high
            v_low[at, :] = low
            v_top[pl.ds(pl.multiple_of(t * top_dom, 8), top_dom), :] = v[box_dom : box_dom + top_dom]
        return carry

    lax.fori_loop(0, n_types // UNROLL, translate, 0)

    sent_top = one_hot_dot(c_top[...].astype(BF16), v_top[...], NN)
    for g in range(groups):
        top_out[g] = sent_top[g : g + 1, :]

    def top_copy(o, source):
        g = lax.rem(me + o, groups)
        return pltpu.make_async_remote_copy(
            src_ref=top_out.at[g],
            dst_ref=top_in.at[source],
            send_sem=top_send.at[o],
            recv_sem=top_recv.at[source],
            device_id=(g // nz, lax.rem(g, nz) * 2 + core),
            device_id_type=MESH,
        )

    for o in range(1, groups):
        top_copy(o, me).start()
    top_in[pl.ds(me, 1)] = top_out[pl.ds(me, 1)]

    hot_leaf = c_leaf[...].astype(BF16)
    sent = dot(hot_leaf, v_high[...], NN) + dot(hot_leaf, v_low[...], NN)
    leaf_out[...] = sent.reshape(3 * nz, 8, sent.shape[1])

    def leaf_copy(w, o, source):
        k = lax.rem(z + o, nz)
        n = w * nz + o
        return pltpu.make_async_remote_copy(
            src_ref=leaf_out.at[w * nz + k],
            dst_ref=leaf_in.at[source],
            send_sem=leaf_send.at[n],
            recv_sem=leaf_recv.at[source],
            device_id=(jnp.clip(s + w - 1, 0, n_space - 1), k * 2 + core),
            device_id_type=MESH,
        )

    has = (s > 0, None, s < n_space - 1)
    for w in (0, 2):
        @pl.when(has[w])
        def _():
            for o in range(nz):
                leaf_copy(w, o, (2 - w) * nz + z).start()
    for o in range(1, nz):
        leaf_copy(1, o, nz + z).start()

    total = jnp.zeros((1, x_ref.shape[1]), F32)
    for o in range(1, groups):
        top_copy(o, lax.rem(me + o, groups)).wait_recv()
    for g in range(groups):
        total += top_in[g]
    total_high, total_low = halves(total)
    stack = jnp.concatenate(
        [total_high.astype(F32), total_low.astype(F32), jnp.zeros((14, total.shape[1]), F32)], axis=0
    ).astype(BF16)
    down = []
    for c in range(8):
        u_high, u_low = halves(u_ref[c])
        both = dot(stack, u_high, NN)
        extra = dot(stack, u_low, NN)
        down.append(both[0:1] + both[1:2] + extra[0:1])
    acc[...] = jnp.concatenate(down, axis=0) + leaf_out[pl.ds(nz + z, 1)][0]
    for o in range(1, nz):
        source = nz + lax.rem(z + o, nz)
        leaf_copy(1, o, source).wait_recv()
        acc[...] += leaf_in[pl.ds(source, 1)][0]
    for w in (0, 2):
        @pl.when(has[w])
        def _():
            for o in range(nz):
                source = w * nz + lax.rem(z + o, nz)
                leaf_copy(w, o, source).wait_recv()
                acc[...] += leaf_in[pl.ds(source, 1)][0]
    mine_ref[...] = acc[...]
    here = pl.ds(j * 8, 8)
    dom[here, :] = acc[...]

    def dom_copy(o, source):
        at = pl.ds(source * 8, 8)
        return pltpu.make_async_remote_copy(
            src_ref=dom.at[at],
            dst_ref=dom.at[at],
            send_sem=dom_send.at[o],
            recv_sem=dom_recv.at[source],
            device_id=(s, lax.rem(j + o, n_blk)),
            device_id_type=MESH,
        )

    for o in range(1, n_blk):
        dom_copy(o, j).start()

    for o in range(1, groups):
        list_copy(o).wait_send()
        top_copy(o, me).wait_send()
    for w in (0, 2):
        @pl.when(has[w])
        def _():
            for o in range(nz):
                leaf_copy(w, o, (2 - w) * nz + z).wait_send()
    for o in range(1, nz):
        leaf_copy(1, o, nz + z).wait_send()

    for o in range(1, n_blk):
        dom_copy(o, lax.rem(j + o, n_blk)).wait_recv()
    rows_ref[...] = one_hot_dot(hot, dom[...], TN)
    for o in range(1, n_blk):
        dom_copy(o, j).wait_send()


def contract(bra, ket, rows_ref, mine_ref, out_hbm, mine_hbm, out, out_sem, mine_sem):
    chunks = bra.shape[0] // GROUP
    mine_copy = pltpu.make_async_copy(mine_ref, mine_hbm, mine_sem)
    mine_copy.start()

    def store(i):
        at = pl.ds(i * GROUP, GROUP)
        return pltpu.make_async_copy(out.at[at], out_hbm.at[at], out_sem.at[i])

    def step(i, carry):
        local = rows_ref[pl.ds(i * GROUP, GROUP), :]
        for first in range(0, GROUP, UNROLL):
            made = []
            for u in range(first, first + UNROLL):
                b = i * GROUP + u
                scaled = (bra[b].astype(F32) * local[u : u + 1, :]).astype(BF16)
                made.append(dot(scaled, ket[b], NT).astype(BF16))
            for u in range(UNROLL):
                out[i * GROUP + first + u] = made[u]
        store(i).start()
        return carry

    lax.fori_loop(0, chunks, step, 0)
    for i in range(chunks):
        store(i).wait()
    mine_copy.wait()


def shards(
    density,
    bra_table,
    ket_table,
    box_of_block,
    leaf_src,
    leaf_type,
    coarse_src,
    coarse_type,
    translation,
    upward_translation_table,
):
    n_space = lax.axis_size("space")
    n_blk = lax.axis_size("blk")
    nz = n_blk // 2
    groups = n_space * nz
    n_blocks, side, coeffs = bra_table.shape
    n_types = translation.shape[0]
    box_dom = 8 * n_blk
    top_dom = n_blk
    chunks = n_blocks // GROUP
    x_rows = -(-(box_dom + top_dom) // 16) * 16
    whole = pl.BlockSpec(memory_space=pltpu.VMEM)
    far = pl.BlockSpec(memory_space=pltpu.HBM)
    dma = pltpu.SemaphoreType.DMA
    ints = jnp.int32
    bra_here, ket_here, rows, mine = pl.pallas_call(
        functools.partial(build, n_space, n_blk, n_types),
        out_shape=(
            jax.ShapeDtypeStruct(bra_table.shape, BF16),
            jax.ShapeDtypeStruct(ket_table.shape, BF16),
            jax.ShapeDtypeStruct((n_blocks, coeffs), F32),
            jax.ShapeDtypeStruct((8, coeffs), F32),
        ),
        in_specs=[far] * 10,
        out_specs=(whole,) * 4,
        scratch_shapes=[
            pltpu.VMEM((1, n_blocks), ints),
            pltpu.VMEM(leaf_src.shape, ints),
            pltpu.VMEM(leaf_type.shape, ints),
            pltpu.VMEM(coarse_src.shape, ints),
            pltpu.VMEM(coarse_type.shape, ints),
            pltpu.VMEM(density.shape, BF16),
            pltpu.VMEM(translation.shape, F32),
            pltpu.VMEM(upward_translation_table.shape, F32),
            pltpu.VMEM((n_blocks, coeffs), F32),
            pltpu.VMEM((box_dom, coeffs), F32),
            pltpu.VMEM((box_dom, coeffs), F32),
            pltpu.VMEM((groups * 16, 128), jnp.int32),
            pltpu.VMEM((3 * nz * 8, n_types * box_dom), F32),
            pltpu.VMEM((groups, n_types * top_dom), F32),
            pltpu.VMEM((x_rows, coeffs), F32),
            pltpu.VMEM((n_types * box_dom, coeffs), BF16),
            pltpu.VMEM((n_types * box_dom, coeffs), BF16),
            pltpu.VMEM((n_types * top_dom, coeffs), F32),
            pltpu.VMEM((3 * nz, 8, coeffs), F32),
            pltpu.VMEM((groups, 1, coeffs), F32),
            pltpu.VMEM((3 * nz, 8, coeffs), F32),
            pltpu.VMEM((groups, 1, coeffs), F32),
            pltpu.VMEM((box_dom, coeffs), F32),
            pltpu.VMEM((8, coeffs), F32),
            pltpu.VMEM((2 * box_dom, coeffs // 2), F32),
            dma((5,)),
            dma((3, chunks)),
            dma((2,)),
            dma((groups,)),
            dma((groups,)),
            dma,
            dma,
            dma((3 * nz,)),
            dma((3 * nz,)),
            dma((groups,)),
            dma((groups,)),
            dma((n_blk,)),
            dma((n_blk,)),
        ],
        compiler_params=pltpu.CompilerParams(
            collective_id=0, has_side_effects=True, vmem_limit_bytes=28 * 1024 * 1024
        ),
        cost_estimate=pl.CostEstimate(
            flops=2 * n_blocks * side * side * coeffs,
            bytes_accessed=22_000_000,
            transcendentals=0,
        ),
    )(
        *(
            pltpu.with_memory_space_constraint(x, pltpu.HBM)
            for x in (
                density,
                bra_table,
                ket_table,
                box_of_block[None, :],
                leaf_src,
                leaf_type,
                coarse_src,
                coarse_type,
                translation,
                upward_translation_table,
            )
        )
    )
    return pl.pallas_call(
        contract,
        out_shape=(
            jax.ShapeDtypeStruct((n_blocks, side, side), BF16),
            jax.ShapeDtypeStruct((8, coeffs), F32),
        ),
        in_specs=[whole] * 4,
        out_specs=(far, far),
        scratch_shapes=[
            pltpu.VMEM((n_blocks, side, side), BF16),
            dma((chunks,)),
            dma,
        ],
        compiler_params=pltpu.CompilerParams(vmem_limit_bytes=16 * 1024 * 1024),
        cost_estimate=pl.CostEstimate(
            flops=2 * n_blocks * side * side * coeffs,
            bytes_accessed=2 * n_blocks * side * side,
            transcendentals=0,
        ),
    )(bra_here, ket_here, rows, mine)


def solution(mesh):
    placed = (
        P(("space", "blk"), None, None),
        P(("space", "blk"), None, None),
        P(("space", "blk"), None, None),
        P(("space", "blk")),
        P(("space", "blk"), None),
        P(("space", "blk"), None),
        P(("space", "blk"), None),
        P(("space", "blk"), None),
        P(),
        P(),
    )
    return jax.shard_map(
        shards,
        mesh=mesh,
        in_specs=placed,
        out_specs=(P(("space", "blk"), None, None), P(("space", "blk"), None)),
        check_vma=False,
    )
```

```python
import functools

import jax
import jax.numpy as jnp
from jax import lax
from jax.experimental import pallas as pl
from jax.experimental.pallas import tpu as pltpu
from jax.sharding import PartitionSpec as P

MESH = pl.DeviceIdType.MESH
F32 = jnp.float32
BF16 = jnp.bfloat16
GROUP = 16
UNROLL = 4
KEY = 1024


def dot(a, b, dims):
    return lax.dot_general(a, b, (dims, ((), ())), preferred_element_type=F32)


NN = ((1,), (0,))
NT = ((1,), (1,))
TN = ((0,), (0,))


def halves(x):
    high = x.astype(BF16)
    return high, (x - high.astype(F32)).astype(BF16)


def one_hot_dot(hot, x, dims):
    high, low = halves(x)
    return dot(hot, high, dims) + dot(hot, low, dims)


def count_hot(keys, width):
    rows, entries = keys.shape
    lane = lax.broadcasted_iota(jnp.int32, (rows, width), 1)
    total = jnp.zeros((rows, width), F32)
    for e in range(entries):
        total += jnp.where(lane == keys[:, e : e + 1], 1.0, 0.0)
    return total


def build(
    n_space,
    n_blk,
    n_types,
    den_hbm, bra_hbm, ket_hbm, box_hbm, lsrc_hbm, ltype_hbm, csrc_hbm, ctype_hbm, t_hbm, u_hbm,
    bra, ket, rows_ref, mine_ref,
    box_ref, lsrc_ref, ltype_ref, csrc_ref, ctype_ref, den, t_ref, u_ref,
    t_high, t_low, u_high, u_low, mom, part, sib, lists, c_leaf, c_top, x_ref, v_high, v_low, v_top,
    leaf_out, top_out, leaf_in, top_in, dom, acc, kids,
    small_sem, load_sem, table_sem, list_send, list_recv, sib_send, sib_recv,
    leaf_send, leaf_recv, top_send, top_recv, dom_send, dom_recv,
):
    s = lax.axis_index("space")
    j = lax.axis_index("blk")
    core = lax.rem(j, 2)
    z = j // 2
    other = j + 1 - 2 * core
    nz = n_blk // 2
    box_dom = 8 * n_blk
    top_dom = n_blk
    n_blocks = den.shape[0]
    chunks = n_blocks // GROUP
    entries = lsrc_ref.shape[1]
    me = s * nz + z
    groups = n_space * nz

    small = [
        pltpu.make_async_copy(src, dst, small_sem.at[k])
        for k, (src, dst) in enumerate(
            (
                (ltype_hbm, ltype_ref),
                (lsrc_hbm, lsrc_ref),
                (ctype_hbm, ctype_ref),
                (csrc_hbm, csrc_ref),
                (box_hbm, box_ref),
            )
        )
    ]

    def loads(i):
        at = pl.ds(i * GROUP, GROUP)
        return [
            pltpu.make_async_copy(src.at[at], dst.at[at], load_sem.at[k, i])
            for k, (src, dst) in enumerate(((den_hbm, den), (ket_hbm, ket), (bra_hbm, bra)))
        ]

    def start_loads(i, carry):
        for copy in loads(i):
            copy.start()
        return carry

    start_loads(0, 0)
    for copy in small:
        copy.start()

    barrier = pltpu.get_barrier_semaphore()
    for o in range(1, groups):
        g = lax.rem(me + o, groups)
        pl.semaphore_signal(
            barrier, inc=1, device_id=(g // nz, lax.rem(g, nz) * 2 + core), device_id_type=MESH
        )
    for k in range(nz):
        pl.semaphore_signal(barrier, inc=1, device_id=(s, k * 2 + 1 - core), device_id_type=MESH)

    lax.fori_loop(1, chunks, start_loads, 0)
    u_copy = pltpu.make_async_copy(u_hbm, u_ref, table_sem.at[0])
    t_copy = pltpu.make_async_copy(t_hbm, t_ref, table_sem.at[1])

    def moments(i):
        for copy in loads(i):
            copy.wait()
        rows = []
        for u in range(GROUP):
            b = i * GROUP + u
            inner = dot(den[b], ket[b], NN)
            rows.append(jnp.sum(inner * bra[b].astype(F32), axis=0, keepdims=True))
        mom[pl.ds(i * GROUP, GROUP), :] = jnp.concatenate(rows, axis=0)

    def counts(n):
        w = n // nz
        target = jnp.clip(s + w - 1, 0, n_space - 1) * nz + lax.rem(n, nz)
        packed = lists[pl.ds(pl.multiple_of(target * 16, 16), 8), 0:entries]
        kind = lax.shift_right_logical(packed, 10)
        place = (packed & (KEY - 1)) - (2 - w) * box_dom
        keys = jnp.where((place >= 0) & (place < box_dom), kind * box_dom + place, -1)
        c_leaf[pl.ds(pl.multiple_of(n * 8, 8), 8), :] = count_hot(keys, n_types * box_dom)

    early = chunks // 2
    each = 3 * nz // (chunks - early)

    def moments_alone(i, carry):
        moments(i)
        return carry

    def moments_and_counts(i, carry):
        moments(i)
        for k in range(each):
            counts((i - early) * each + k)
        return carry

    lax.fori_loop(0, 1, moments_alone, 0)
    u_copy.start()
    t_copy.start()

    for copy in small:
        copy.wait()
    lists[pl.ds(me * 16, 8), 0:entries] = ltype_ref[...] * KEY + lsrc_ref[...]
    lists[pl.ds(me * 16 + 8, 1), 0:entries] = ctype_ref[...] * KEY + csrc_ref[...]
    pl.semaphore_wait(barrier, groups - 1 + nz)

    def list_copy(o):
        g = lax.rem(me + o, groups)
        at = pl.ds(me * 16, 16)
        return pltpu.make_async_remote_copy(
            src_ref=lists.at[at],
            dst_ref=lists.at[at],
            send_sem=list_send.at[o],
            recv_sem=list_recv.at[me],
            device_id=(g // nz, lax.rem(g, nz) * 2 + core),
            device_id_type=MESH,
        )

    def list_arrival(o):
        g = lax.rem(me + o, groups)
        at = pl.ds(g * 16, 16)
        return pltpu.make_async_remote_copy(
            src_ref=lists.at[at],
            dst_ref=lists.at[at],
            send_sem=list_send.at[o],
            recv_sem=list_recv.at[g],
            device_id=(g // nz, lax.rem(g, nz) * 2 + core),
            device_id_type=MESH,
        )

    for o in range(1, groups):
        list_copy(o).start()

    lax.fori_loop(1, early, moments_alone, 0)
    for o in range(1, groups):
        list_arrival(o).wait_recv()
    lax.fori_loop(early, chunks, moments_and_counts, 0)
    hot = jnp.where(
        lax.broadcasted_iota(jnp.int32, (box_dom, n_blocks), 0) == box_ref[...], 1.0, 0.0
    ).astype(BF16)
    part[...] = one_hot_dot(hot, mom[...], NN)

    sib_copy = pltpu.make_async_remote_copy(
        src_ref=part,
        dst_ref=sib,
        send_sem=sib_send,
        recv_sem=sib_recv,
        device_id=(s, other),
        device_id_type=MESH,
    )
    sib_copy.start()

    packed = lists[pl.ds(8, groups, stride=16), :]
    kind = lax.shift_right_logical(packed, 10)
    place = (packed & (KEY - 1)) - s * top_dom
    keys = jnp.where((place >= 0) & (place < top_dom), kind * top_dom + place, -1)
    c_top[...] = count_hot(keys[:, 0:entries], n_types * top_dom)

    u_copy.wait()
    t_copy.wait()

    def split_table(i, carry):
        high, low = halves(t_ref[i])
        t_high[i] = high
        t_low[i] = low

        @pl.when(i < 8)
        def _():
            high, low = halves(u_ref[i])
            u_high[i] = high
            u_low[i] = low

        return carry

    lax.fori_loop(0, n_types, split_table, 0)
    sib_copy.wait()
    own = part[...] + sib[...]
    x_ref[0:box_dom, :] = own
    kids[0:box_dom, :] = own[:, 0:128]
    kids[box_dom:, :] = own[:, 128:]
    x_ref[box_dom:, :] = jnp.zeros((x_ref.shape[0] - box_dom, x_ref.shape[1]), F32)

    tops = jnp.zeros((top_dom, x_ref.shape[1]), F32)
    for c in range(8):
        child = jnp.concatenate(
            [kids[pl.ds(h * box_dom + c, top_dom, stride=8), :] for h in range(2)], axis=1
        )
        c_high, c_low = halves(child)
        stack = jnp.concatenate([c_high.astype(F32), c_low.astype(F32)], axis=0).astype(BF16)
        both = dot(stack, u_high[c], NT)
        extra = dot(stack, u_low[c], NT)
        tops += both[:top_dom] + both[top_dom:] + extra[:top_dom]
    x_ref[box_dom : box_dom + top_dom, :] = tops

    x = x_ref[...]
    x_high, x_low = halves(x)
    x_rows = x.shape[0]
    stack = jnp.concatenate([x_high, x_low], axis=0)
    for t in range(n_types):
        both = dot(stack, t_high[t], NT)
        v = both[:x_rows] + both[x_rows:] + dot(x_high, t_low[t], NT)
        high, low = halves(v[:box_dom])
        v_high[t * box_dom : (t + 1) * box_dom, :] = high
        v_low[t * box_dom : (t + 1) * box_dom, :] = low
        v_top[t * top_dom : (t + 1) * top_dom, :] = v[box_dom : box_dom + top_dom]

    sent_top = one_hot_dot(c_top[...].astype(BF16), v_top[...], NN)
    for g in range(groups):
        top_out[g] = sent_top[g : g + 1, :]

    def top_copy(o, source):
        g = lax.rem(me + o, groups)
        return pltpu.make_async_remote_copy(
            src_ref=top_out.at[g],
            dst_ref=top_in.at[source],
            send_sem=top_send.at[o],
            recv_sem=top_recv.at[source],
            device_id=(g // nz, lax.rem(g, nz) * 2 + core),
            device_id_type=MESH,
        )

    for o in range(1, groups):
        top_copy(o, me).start()
    top_in[pl.ds(me, 1)] = top_out[pl.ds(me, 1)]

    hot_leaf = c_leaf[...].astype(BF16)
    sent = dot(hot_leaf, v_high[...], NN) + dot(hot_leaf, v_low[...], NN)
    leaf_out[...] = sent.reshape(3 * nz, 8, sent.shape[1])

    def leaf_copy(w, o, source):
        k = lax.rem(z + o, nz)
        n = w * nz + o
        return pltpu.make_async_remote_copy(
            src_ref=leaf_out.at[w * nz + k],
            dst_ref=leaf_in.at[source],
            send_sem=leaf_send.at[n],
            recv_sem=leaf_recv.at[source],
            device_id=(jnp.clip(s + w - 1, 0, n_space - 1), k * 2 + core),
            device_id_type=MESH,
        )

    has = (s > 0, None, s < n_space - 1)
    for w in (0, 2):
        @pl.when(has[w])
        def _():
            for o in range(nz):
                leaf_copy(w, o, (2 - w) * nz + z).start()
    for o in range(1, nz):
        leaf_copy(1, o, nz + z).start()

    total = jnp.zeros((1, x_ref.shape[1]), F32)
    for o in range(1, groups):
        top_copy(o, lax.rem(me + o, groups)).wait_recv()
    for g in range(groups):
        total += top_in[g]
    total_high, total_low = halves(total)
    stack = jnp.concatenate(
        [total_high.astype(F32), total_low.astype(F32), jnp.zeros((14, total.shape[1]), F32)], axis=0
    ).astype(BF16)
    down = []
    for c in range(8):
        both = dot(stack, u_high[c], NN)
        extra = dot(stack, u_low[c], NN)
        down.append(both[0:1] + both[1:2] + extra[0:1])
    acc[...] = jnp.concatenate(down, axis=0) + leaf_out[pl.ds(nz + z, 1)][0]
    for o in range(1, nz):
        source = nz + lax.rem(z + o, nz)
        leaf_copy(1, o, source).wait_recv()
        acc[...] += leaf_in[pl.ds(source, 1)][0]
    for w in (0, 2):
        @pl.when(has[w])
        def _():
            for o in range(nz):
                source = w * nz + lax.rem(z + o, nz)
                leaf_copy(w, o, source).wait_recv()
                acc[...] += leaf_in[pl.ds(source, 1)][0]
    mine_ref[...] = acc[...]
    here = pl.ds(j * 8, 8)
    dom[here, :] = acc[...]

    def dom_copy(o, source):
        at = pl.ds(source * 8, 8)
        return pltpu.make_async_remote_copy(
            src_ref=dom.at[at],
            dst_ref=dom.at[at],
            send_sem=dom_send.at[o],
            recv_sem=dom_recv.at[source],
            device_id=(s, lax.rem(j + o, n_blk)),
            device_id_type=MESH,
        )

    for o in range(1, n_blk):
        dom_copy(o, j).start()

    for o in range(1, groups):
        list_copy(o).wait_send()
        top_copy(o, me).wait_send()
    for w in (0, 2):
        @pl.when(has[w])
        def _():
            for o in range(nz):
                leaf_copy(w, o, (2 - w) * nz + z).wait_send()
    for o in range(1, nz):
        leaf_copy(1, o, nz + z).wait_send()

    for o in range(1, n_blk):
        dom_copy(o, lax.rem(j + o, n_blk)).wait_recv()
    rows_ref[...] = one_hot_dot(hot, dom[...], TN)
    for o in range(1, n_blk):
        dom_copy(o, j).wait_send()


def contract(bra, ket, rows_ref, mine_ref, out_hbm, mine_hbm, out, out_sem, mine_sem):
    chunks = bra.shape[0] // GROUP
    mine_copy = pltpu.make_async_copy(mine_ref, mine_hbm, mine_sem)
    mine_copy.start()

    def store(i):
        at = pl.ds(i * GROUP, GROUP)
        return pltpu.make_async_copy(out.at[at], out_hbm.at[at], out_sem.at[i])

    def step(i, carry):
        local = rows_ref[pl.ds(i * GROUP, GROUP), :]
        for first in range(0, GROUP, UNROLL):
            made = []
            for u in range(first, first + UNROLL):
                b = i * GROUP + u
                scaled = (bra[b].astype(F32) * local[u : u + 1, :]).astype(BF16)
                made.append(dot(scaled, ket[b], NT).astype(BF16))
            for u in range(UNROLL):
                out[i * GROUP + first + u] = made[u]
        store(i).start()
        return carry

    lax.fori_loop(0, chunks, step, 0)
    for i in range(chunks):
        store(i).wait()
    mine_copy.wait()


def shards(
    density,
    bra_table,
    ket_table,
    box_of_block,
    leaf_src,
    leaf_type,
    coarse_src,
    coarse_type,
    translation,
    upward_translation_table,
):
    n_space = lax.axis_size("space")
    n_blk = lax.axis_size("blk")
    nz = n_blk // 2
    groups = n_space * nz
    n_blocks, side, coeffs = bra_table.shape
    n_types = translation.shape[0]
    box_dom = 8 * n_blk
    top_dom = n_blk
    chunks = n_blocks // GROUP
    x_rows = -(-(box_dom + top_dom) // 16) * 16
    whole = pl.BlockSpec(memory_space=pltpu.VMEM)
    far = pl.BlockSpec(memory_space=pltpu.HBM)
    dma = pltpu.SemaphoreType.DMA
    ints = jnp.int32
    bra_here, ket_here, rows, mine = pl.pallas_call(
        functools.partial(build, n_space, n_blk, n_types),
        out_shape=(
            jax.ShapeDtypeStruct(bra_table.shape, BF16),
            jax.ShapeDtypeStruct(ket_table.shape, BF16),
            jax.ShapeDtypeStruct((n_blocks, coeffs), F32),
            jax.ShapeDtypeStruct((8, coeffs), F32),
        ),
        in_specs=[far] * 10,
        out_specs=(whole,) * 4,
        scratch_shapes=[
            pltpu.VMEM((1, n_blocks), ints),
            pltpu.VMEM(leaf_src.shape, ints),
            pltpu.VMEM(leaf_type.shape, ints),
            pltpu.VMEM(coarse_src.shape, ints),
            pltpu.VMEM(coarse_type.shape, ints),
            pltpu.VMEM(density.shape, BF16),
            pltpu.VMEM(translation.shape, F32),
            pltpu.VMEM(upward_translation_table.shape, F32),
            pltpu.VMEM(translation.shape, BF16),
            pltpu.VMEM(translation.shape, BF16),
            pltpu.VMEM(upward_translation_table.shape, BF16),
            pltpu.VMEM(upward_translation_table.shape, BF16),
            pltpu.VMEM((n_blocks, coeffs), F32),
            pltpu.VMEM((box_dom, coeffs), F32),
            pltpu.VMEM((box_dom, coeffs), F32),
            pltpu.VMEM((groups * 16, 128), jnp.int32),
            pltpu.VMEM((3 * nz * 8, n_types * box_dom), F32),
            pltpu.VMEM((groups, n_types * top_dom), F32),
            pltpu.VMEM((x_rows, coeffs), F32),
            pltpu.VMEM((n_types * box_dom, coeffs), BF16),
            pltpu.VMEM((n_types * box_dom, coeffs), BF16),
            pltpu.VMEM((n_types * top_dom, coeffs), F32),
            pltpu.VMEM((3 * nz, 8, coeffs), F32),
            pltpu.VMEM((groups, 1, coeffs), F32),
            pltpu.VMEM((3 * nz, 8, coeffs), F32),
            pltpu.VMEM((groups, 1, coeffs), F32),
            pltpu.VMEM((box_dom, coeffs), F32),
            pltpu.VMEM((8, coeffs), F32),
            pltpu.VMEM((2 * box_dom, coeffs // 2), F32),
            dma((5,)),
            dma((3, chunks)),
            dma((2,)),
            dma((groups,)),
            dma((groups,)),
            dma,
            dma,
            dma((3 * nz,)),
            dma((3 * nz,)),
            dma((groups,)),
            dma((groups,)),
            dma((n_blk,)),
            dma((n_blk,)),
        ],
        compiler_params=pltpu.CompilerParams(
            collective_id=0, has_side_effects=True, vmem_limit_bytes=32 * 1024 * 1024
        ),
        cost_estimate=pl.CostEstimate(
            flops=2 * n_blocks * side * side * coeffs,
            bytes_accessed=22_000_000,
            transcendentals=0,
        ),
    )(
        *(
            pltpu.with_memory_space_constraint(x, pltpu.HBM)
            for x in (
                density,
                bra_table,
                ket_table,
                box_of_block[None, :],
                leaf_src,
                leaf_type,
                coarse_src,
                coarse_type,
                translation,
                upward_translation_table,
            )
        )
    )
    return pl.pallas_call(
        contract,
        out_shape=(
            jax.ShapeDtypeStruct((n_blocks, side, side), BF16),
            jax.ShapeDtypeStruct((8, coeffs), F32),
        ),
        in_specs=[whole] * 4,
        out_specs=(far, far),
        scratch_shapes=[
            pltpu.VMEM((n_blocks, side, side), BF16),
            dma((chunks,)),
            dma,
        ],
        compiler_params=pltpu.CompilerParams(vmem_limit_bytes=16 * 1024 * 1024),
        cost_estimate=pl.CostEstimate(
            flops=2 * n_blocks * side * side * coeffs,
            bytes_accessed=2 * n_blocks * side * side,
            transcendentals=0,
        ),
    )(bra_here, ket_here, rows, mine)


def solution(mesh):
    placed = (
        P(("space", "blk"), None, None),
        P(("space", "blk"), None, None),
        P(("space", "blk"), None, None),
        P(("space", "blk")),
        P(("space", "blk"), None),
        P(("space", "blk"), None),
        P(("space", "blk"), None),
        P(("space", "blk"), None),
        P(),
        P(),
    )
    return jax.shard_map(
        shards,
        mesh=mesh,
        in_specs=placed,
        out_specs=(P(("space", "blk"), None, None), P(("space", "blk"), None)),
        check_vma=False,
    )
```

```python
import functools

import jax
import jax.numpy as jnp
from jax import lax
from jax.experimental import pallas as pl
from jax.experimental.pallas import tpu as pltpu
from jax.sharding import PartitionSpec as P

MESH = pl.DeviceIdType.MESH
F32 = jnp.float32
BF16 = jnp.bfloat16
GROUP = 8
STEP = 16
PIECES = 4
KEY = 1024


def dot(a, b, dims):
    return lax.dot_general(a, b, (dims, ((), ())), preferred_element_type=F32)


NN = ((1,), (0,))
NT = ((1,), (1,))
TN = ((0,), (0,))


def halves(x):
    high = x.astype(BF16)
    return high, (x - high.astype(F32)).astype(BF16)


def one_hot_dot(hot, x, dims):
    high, low = halves(x)
    return dot(hot, high, dims) + dot(hot, low, dims)


def count_hot(keys, width):
    rows, entries = keys.shape
    lane = lax.broadcasted_iota(jnp.int32, (rows, width), 1)
    total = jnp.zeros((rows, width), F32)
    for e in range(entries):
        total += jnp.where(lane == keys[:, e : e + 1], 1.0, 0.0)
    return total


def build(
    n_space,
    n_blk,
    n_types,
    den_hbm, bra_hbm, ket_hbm, box_hbm, lsrc_hbm, ltype_hbm, csrc_hbm, ctype_hbm, t_hbm, u_hbm,
    bra, ket, rows_ref, mine_ref,
    box_ref, lsrc_ref, ltype_ref, csrc_ref, ctype_ref, den, t_ref, u_ref, mom, part, sib, lists, c_leaf, c_top, x_ref, v_high, v_low, v_top,
    leaf_out, top_out, leaf_in, top_in, dom, acc, kids,
    small_sem, load_sem, table_sem, list_send, list_recv, sib_send, sib_recv,
    leaf_send, leaf_recv, top_send, top_recv, dom_send, dom_recv,
):
    s = lax.axis_index("space")
    j = lax.axis_index("blk")
    core = lax.rem(j, 2)
    z = j // 2
    other = j + 1 - 2 * core
    nz = n_blk // 2
    box_dom = 8 * n_blk
    top_dom = n_blk
    n_blocks = den.shape[0]
    chunks = n_blocks // GROUP
    entries = lsrc_ref.shape[1]
    me = s * nz + z
    groups = n_space * nz

    small = [
        pltpu.make_async_copy(src, dst, small_sem.at[k])
        for k, (src, dst) in enumerate(
            (
                (ltype_hbm, ltype_ref),
                (lsrc_hbm, lsrc_ref),
                (ctype_hbm, ctype_ref),
                (csrc_hbm, csrc_ref),
                (box_hbm, box_ref),
            )
        )
    ]

    def loads(i):
        at = pl.ds(i * GROUP, GROUP)
        return [
            pltpu.make_async_copy(src.at[at], dst.at[at], load_sem.at[k, i])
            for k, (src, dst) in enumerate(((den_hbm, den), (ket_hbm, ket), (bra_hbm, bra)))
        ]

    def start_loads(i, carry):
        for copy in loads(i):
            copy.start()
        return carry

    start_loads(0, 0)
    for copy in small:
        copy.start()

    barrier = pltpu.get_barrier_semaphore()
    for o in range(1, groups):
        g = lax.rem(me + o, groups)
        pl.semaphore_signal(
            barrier, inc=1, device_id=(g // nz, lax.rem(g, nz) * 2 + core), device_id_type=MESH
        )
    for k in range(nz):
        pl.semaphore_signal(barrier, inc=1, device_id=(s, k * 2 + 1 - core), device_id_type=MESH)

    lax.fori_loop(1, chunks, start_loads, 0)
    u_copy = pltpu.make_async_copy(u_hbm, u_ref, table_sem.at[0])
    u_copy.start()
    piece = n_types // PIECES
    t_copies = []
    for i in range(PIECES):
        at = pl.ds(i * piece, piece)
        t_copies.append(pltpu.make_async_copy(t_hbm.at[at], t_ref.at[at], table_sem.at[1 + i]))
        t_copies[i].start()

    def moments(i, carry):
        for copy in loads(i):
            copy.wait()
        rows = []
        for u in range(GROUP):
            b = i * GROUP + u
            inner = dot(den[b], ket[b], NN)
            rows.append(jnp.sum(inner * bra[b].astype(F32), axis=0, keepdims=True))
        mom[pl.ds(i * GROUP, GROUP), :] = jnp.concatenate(rows, axis=0)
        return carry

    lax.fori_loop(0, chunks // 2, moments, 0)

    for copy in small:
        copy.wait()
    lists[pl.ds(me * 16, 8), 0:entries] = ltype_ref[...] * KEY + lsrc_ref[...]
    lists[pl.ds(me * 16 + 8, 1), 0:entries] = ctype_ref[...] * KEY + csrc_ref[...]
    pl.semaphore_wait(barrier, groups - 1 + nz)

    def list_copy(o):
        g = lax.rem(me + o, groups)
        at = pl.ds(me * 16, 16)
        return pltpu.make_async_remote_copy(
            src_ref=lists.at[at],
            dst_ref=lists.at[at],
            send_sem=list_send.at[o],
            recv_sem=list_recv.at[me],
            device_id=(g // nz, lax.rem(g, nz) * 2 + core),
            device_id_type=MESH,
        )

    def list_arrival(o):
        g = lax.rem(me + o, groups)
        at = pl.ds(g * 16, 16)
        return pltpu.make_async_remote_copy(
            src_ref=lists.at[at],
            dst_ref=lists.at[at],
            send_sem=list_send.at[o],
            recv_sem=list_recv.at[g],
            device_id=(g // nz, lax.rem(g, nz) * 2 + core),
            device_id_type=MESH,
        )

    for o in range(1, groups):
        list_copy(o).start()

    lax.fori_loop(chunks // 2, chunks, moments, 0)
    hot = jnp.where(
        lax.broadcasted_iota(jnp.int32, (box_dom, n_blocks), 0) == box_ref[...], 1.0, 0.0
    ).astype(BF16)
    part[...] = one_hot_dot(hot, mom[...], NN)

    sib_copy = pltpu.make_async_remote_copy(
        src_ref=part,
        dst_ref=sib,
        send_sem=sib_send,
        recv_sem=sib_recv,
        device_id=(s, other),
        device_id_type=MESH,
    )
    sib_copy.start()

    for o in range(1, groups):
        list_arrival(o).wait_recv()
    for w in range(3):
        sender_at = 2 - w
        target = jnp.clip(s + w - 1, 0, n_space - 1)
        for k in range(nz):
            packed = lists[pl.ds((target * nz + k) * 16, 8), 0:entries]
            kind = lax.shift_right_logical(packed, 10)
            place = (packed & (KEY - 1)) - sender_at * box_dom
            keys = jnp.where((place >= 0) & (place < box_dom), kind * box_dom + place, -1)
            c_leaf[pl.ds((w * nz + k) * 8, 8), :] = count_hot(keys, n_types * box_dom)
    packed = lists[pl.ds(8, groups, stride=16), :]
    kind = lax.shift_right_logical(packed, 10)
    place = (packed & (KEY - 1)) - s * top_dom
    keys = jnp.where((place >= 0) & (place < top_dom), kind * top_dom + place, -1)
    c_top[...] = count_hot(keys[:, 0:entries], n_types * top_dom)

    u_copy.wait()
    sib_copy.wait()
    own = part[...] + sib[...]
    x_ref[0:box_dom, :] = own
    kids[0:box_dom, :] = own[:, 0:128]
    kids[box_dom:, :] = own[:, 128:]
    x_ref[box_dom:, :] = jnp.zeros((x_ref.shape[0] - box_dom, x_ref.shape[1]), F32)

    tops = jnp.zeros((top_dom, x_ref.shape[1]), F32)
    for c in range(8):
        child = jnp.concatenate(
            [kids[pl.ds(h * box_dom + c, top_dom, stride=8), :] for h in range(2)], axis=1
        )
        c_high, c_low = halves(child)
        stack = jnp.concatenate([c_high.astype(F32), c_low.astype(F32)], axis=0).astype(BF16)
        u_high, u_low = halves(u_ref[c])
        both = dot(stack, u_high, NT)
        extra = dot(stack, u_low, NT)
        tops += both[:top_dom] + both[top_dom:] + extra[:top_dom]
    x_ref[box_dom : box_dom + top_dom, :] = tops

    x = x_ref[...]
    x_high, x_low = halves(x)
    x_rows = x.shape[0]
    stack = jnp.concatenate([x_high, x_low], axis=0)
    for t in range(n_types):
        if t % piece == 0:
            t_copies[t // piece].wait()
        t_high, t_low = halves(t_ref[t])
        both = dot(stack, t_high, NT)
        v = both[:x_rows] + both[x_rows:] + dot(x_high, t_low, NT)
        high, low = halves(v[:box_dom])
        v_high[t * box_dom : (t + 1) * box_dom, :] = high
        v_low[t * box_dom : (t + 1) * box_dom, :] = low
        v_top[t * top_dom : (t + 1) * top_dom, :] = v[box_dom : box_dom + top_dom]

    sent_top = one_hot_dot(c_top[...].astype(BF16), v_top[...], NN)
    for g in range(groups):
        top_out[g] = sent_top[g : g + 1, :]

    def top_copy(o, source):
        g = lax.rem(me + o, groups)
        return pltpu.make_async_remote_copy(
            src_ref=top_out.at[g],
            dst_ref=top_in.at[source],
            send_sem=top_send.at[o],
            recv_sem=top_recv.at[source],
            device_id=(g // nz, lax.rem(g, nz) * 2 + core),
            device_id_type=MESH,
        )

    for o in range(1, groups):
        top_copy(o, me).start()
    top_in[pl.ds(me, 1)] = top_out[pl.ds(me, 1)]

    hot_leaf = c_leaf[...].astype(BF16)
    sent = dot(hot_leaf, v_high[...], NN) + dot(hot_leaf, v_low[...], NN)
    leaf_out[...] = sent.reshape(3 * nz, 8, sent.shape[1])

    def leaf_copy(w, o, source):
        k = lax.rem(z + o, nz)
        n = w * nz + o
        return pltpu.make_async_remote_copy(
            src_ref=leaf_out.at[w * nz + k],
            dst_ref=leaf_in.at[source],
            send_sem=leaf_send.at[n],
            recv_sem=leaf_recv.at[source],
            device_id=(jnp.clip(s + w - 1, 0, n_space - 1), k * 2 + core),
            device_id_type=MESH,
        )

    has = (s > 0, None, s < n_space - 1)
    for w in (0, 2):
        @pl.when(has[w])
        def _():
            for o in range(nz):
                leaf_copy(w, o, (2 - w) * nz + z).start()
    for o in range(1, nz):
        leaf_copy(1, o, nz + z).start()

    total = jnp.zeros((1, x_ref.shape[1]), F32)
    for o in range(1, groups):
        top_copy(o, lax.rem(me + o, groups)).wait_recv()
    for g in range(groups):
        total += top_in[g]
    total_high, total_low = halves(total)
    stack = jnp.concatenate(
        [total_high.astype(F32), total_low.astype(F32), jnp.zeros((14, total.shape[1]), F32)], axis=0
    ).astype(BF16)
    down = []
    for c in range(8):
        u_high, u_low = halves(u_ref[c])
        both = dot(stack, u_high, NN)
        extra = dot(stack, u_low, NN)
        down.append(both[0:1] + both[1:2] + extra[0:1])
    acc[...] = jnp.concatenate(down, axis=0) + leaf_out[pl.ds(nz + z, 1)][0]
    for o in range(1, nz):
        source = nz + lax.rem(z + o, nz)
        leaf_copy(1, o, source).wait_recv()
        acc[...] += leaf_in[pl.ds(source, 1)][0]
    for w in (0, 2):
        @pl.when(has[w])
        def _():
            for o in range(nz):
                source = w * nz + lax.rem(z + o, nz)
                leaf_copy(w, o, source).wait_recv()
                acc[...] += leaf_in[pl.ds(source, 1)][0]
    mine_ref[...] = acc[...]
    here = pl.ds(j * 8, 8)
    dom[here, :] = acc[...]

    def dom_copy(o, source):
        at = pl.ds(source * 8, 8)
        return pltpu.make_async_remote_copy(
            src_ref=dom.at[at],
            dst_ref=dom.at[at],
            send_sem=dom_send.at[o],
            recv_sem=dom_recv.at[source],
            device_id=(s, lax.rem(j + o, n_blk)),
            device_id_type=MESH,
        )

    for o in range(1, n_blk):
        dom_copy(o, j).start()

    for o in range(1, groups):
        list_copy(o).wait_send()
        top_copy(o, me).wait_send()
    for w in (0, 2):
        @pl.when(has[w])
        def _():
            for o in range(nz):
                leaf_copy(w, o, (2 - w) * nz + z).wait_send()
    for o in range(1, nz):
        leaf_copy(1, o, nz + z).wait_send()

    for o in range(1, n_blk):
        dom_copy(o, lax.rem(j + o, n_blk)).wait_recv()
    rows_ref[...] = one_hot_dot(hot, dom[...], TN)
    for o in range(1, n_blk):
        dom_copy(o, j).wait_send()


def contract(bra, ket, rows_ref, mine_ref, out_hbm, mine_hbm, out, out_sem, mine_sem):
    mine_copy = pltpu.make_async_copy(mine_ref, mine_hbm, mine_sem)
    mine_copy.start()

    def store(i):
        at = pl.ds(i * STEP, STEP)
        return pltpu.make_async_copy(out.at[at], out_hbm.at[at], out_sem.at[i])

    def step(i, carry):
        local = rows_ref[pl.ds(i * STEP, STEP), :]
        for first in range(0, STEP, 4):
            made = []
            for u in range(first, first + 4):
                b = i * STEP + u
                scaled = (bra[b].astype(F32) * local[u : u + 1, :]).astype(BF16)
                made.append(dot(scaled, ket[b], NT).astype(BF16))
            for u in range(4):
                out[i * STEP + first + u] = made[u]
        store(i).start()
        return carry

    steps = bra.shape[0] // STEP
    lax.fori_loop(0, steps, step, 0)
    for i in range(steps):
        store(i).wait()
    mine_copy.wait()


def shards(
    density,
    bra_table,
    ket_table,
    box_of_block,
    leaf_src,
    leaf_type,
    coarse_src,
    coarse_type,
    translation,
    upward_translation_table,
):
    n_space = lax.axis_size("space")
    n_blk = lax.axis_size("blk")
    nz = n_blk // 2
    groups = n_space * nz
    n_blocks, side, coeffs = bra_table.shape
    n_types = translation.shape[0]
    box_dom = 8 * n_blk
    top_dom = n_blk
    chunks = n_blocks // GROUP
    x_rows = -(-(box_dom + top_dom) // 16) * 16
    whole = pl.BlockSpec(memory_space=pltpu.VMEM)
    far = pl.BlockSpec(memory_space=pltpu.HBM)
    dma = pltpu.SemaphoreType.DMA
    ints = jnp.int32
    bra_here, ket_here, rows, mine = pl.pallas_call(
        functools.partial(build, n_space, n_blk, n_types),
        out_shape=(
            jax.ShapeDtypeStruct(bra_table.shape, BF16),
            jax.ShapeDtypeStruct(ket_table.shape, BF16),
            jax.ShapeDtypeStruct((n_blocks, coeffs), F32),
            jax.ShapeDtypeStruct((8, coeffs), F32),
        ),
        in_specs=[far] * 10,
        out_specs=(whole,) * 4,
        scratch_shapes=[
            pltpu.VMEM((1, n_blocks), ints),
            pltpu.VMEM(leaf_src.shape, ints),
            pltpu.VMEM(leaf_type.shape, ints),
            pltpu.VMEM(coarse_src.shape, ints),
            pltpu.VMEM(coarse_type.shape, ints),
            pltpu.VMEM(density.shape, BF16),
            pltpu.VMEM(translation.shape, F32),
            pltpu.VMEM(upward_translation_table.shape, F32),
            pltpu.VMEM((n_blocks, coeffs), F32),
            pltpu.VMEM((box_dom, coeffs), F32),
            pltpu.VMEM((box_dom, coeffs), F32),
            pltpu.VMEM((groups * 16, 128), jnp.int32),
            pltpu.VMEM((3 * nz * 8, n_types * box_dom), F32),
            pltpu.VMEM((groups, n_types * top_dom), F32),
            pltpu.VMEM((x_rows, coeffs), F32),
            pltpu.VMEM((n_types * box_dom, coeffs), BF16),
            pltpu.VMEM((n_types * box_dom, coeffs), BF16),
            pltpu.VMEM((n_types * top_dom, coeffs), F32),
            pltpu.VMEM((3 * nz, 8, coeffs), F32),
            pltpu.VMEM((groups, 1, coeffs), F32),
            pltpu.VMEM((3 * nz, 8, coeffs), F32),
            pltpu.VMEM((groups, 1, coeffs), F32),
            pltpu.VMEM((box_dom, coeffs), F32),
            pltpu.VMEM((8, coeffs), F32),
            pltpu.VMEM((2 * box_dom, coeffs // 2), F32),
            dma((5,)),
            dma((3, chunks)),
            dma((1 + PIECES,)),
            dma((groups,)),
            dma((groups,)),
            dma,
            dma,
            dma((3 * nz,)),
            dma((3 * nz,)),
            dma((groups,)),
            dma((groups,)),
            dma((n_blk,)),
            dma((n_blk,)),
        ],
        compiler_params=pltpu.CompilerParams(
            collective_id=0, has_side_effects=True, vmem_limit_bytes=28 * 1024 * 1024
        ),
        cost_estimate=pl.CostEstimate(
            flops=2 * n_blocks * side * side * coeffs,
            bytes_accessed=22_000_000,
            transcendentals=0,
        ),
    )(
        *(
            pltpu.with_memory_space_constraint(x, pltpu.HBM)
            for x in (
                density,
                bra_table,
                ket_table,
                box_of_block[None, :],
                leaf_src,
                leaf_type,
                coarse_src,
                coarse_type,
                translation,
                upward_translation_table,
            )
        )
    )
    return pl.pallas_call(
        contract,
        out_shape=(
            jax.ShapeDtypeStruct((n_blocks, side, side), BF16),
            jax.ShapeDtypeStruct((8, coeffs), F32),
        ),
        in_specs=[whole] * 4,
        out_specs=(far, far),
        scratch_shapes=[
            pltpu.VMEM((n_blocks, side, side), BF16),
            dma((n_blocks // STEP,)),
            dma,
        ],
        compiler_params=pltpu.CompilerParams(vmem_limit_bytes=16 * 1024 * 1024),
        cost_estimate=pl.CostEstimate(
            flops=2 * n_blocks * side * side * coeffs,
            bytes_accessed=2 * n_blocks * side * side,
            transcendentals=0,
        ),
    )(bra_here, ket_here, rows, mine)


def solution(mesh):
    placed = (
        P(("space", "blk"), None, None),
        P(("space", "blk"), None, None),
        P(("space", "blk"), None, None),
        P(("space", "blk")),
        P(("space", "blk"), None),
        P(("space", "blk"), None),
        P(("space", "blk"), None),
        P(("space", "blk"), None),
        P(),
        P(),
    )
    return jax.shard_map(
        shards,
        mesh=mesh,
        in_specs=placed,
        out_specs=(P(("space", "blk"), None, None), P(("space", "blk"), None)),
        check_vma=False,
    )
```

```python
import functools

import jax
import jax.numpy as jnp
from jax import lax
from jax.experimental import pallas as pl
from jax.experimental.pallas import tpu as pltpu
from jax.sharding import PartitionSpec as P

MESH = pl.DeviceIdType.MESH
F32 = jnp.float32
BF16 = jnp.bfloat16
GROUP = 8
STEP = 16
PIECES = 4
KEY = 1024


def dot(a, b, dims):
    return lax.dot_general(a, b, (dims, ((), ())), preferred_element_type=F32)


NN = ((1,), (0,))
NT = ((1,), (1,))
TN = ((0,), (0,))


def halves(x):
    high = x.astype(BF16)
    return high, (x - high.astype(F32)).astype(BF16)


def one_hot_dot(hot, x, dims):
    high, low = halves(x)
    return dot(hot, high, dims) + dot(hot, low, dims)


def count_hot(keys, width):
    rows, entries = keys.shape
    lane = lax.broadcasted_iota(jnp.int32, (rows, width), 1)
    total = jnp.zeros((rows, width), F32)
    for e in range(entries):
        total += jnp.where(lane == keys[:, e : e + 1], 1.0, 0.0)
    return total


def build(
    n_space,
    n_blk,
    n_types,
    den_hbm, bra_hbm, ket_hbm, box_hbm, lsrc_hbm, ltype_hbm, csrc_hbm, ctype_hbm, t_hbm, u_hbm,
    bra, ket, rows_ref, mine_ref,
    box_ref, lsrc_ref, ltype_ref, csrc_ref, ctype_ref, den, t_ref, u_ref, mom, part, sib, lists, c_leaf, c_top, x_ref, v_high, v_low, v_top,
    leaf_out, top_out, leaf_in, top_in, dom, acc, kids, hot_rows,
    small_sem, load_sem, table_sem, list_send, list_recv, sib_send, sib_recv,
    leaf_send, leaf_recv, top_send, top_recv, dom_send, dom_recv,
):
    s = lax.axis_index("space")
    j = lax.axis_index("blk")
    core = lax.rem(j, 2)
    z = j // 2
    other = j + 1 - 2 * core
    nz = n_blk // 2
    box_dom = 8 * n_blk
    top_dom = n_blk
    n_blocks = den.shape[0]
    chunks = n_blocks // GROUP
    entries = lsrc_ref.shape[1]
    me = s * nz + z
    groups = n_space * nz

    small = [
        pltpu.make_async_copy(src, dst, small_sem.at[k])
        for k, (src, dst) in enumerate(
            (
                (ltype_hbm, ltype_ref),
                (lsrc_hbm, lsrc_ref),
                (ctype_hbm, ctype_ref),
                (csrc_hbm, csrc_ref),
                (box_hbm, box_ref),
            )
        )
    ]

    def loads(i):
        at = pl.ds(i * GROUP, GROUP)
        return [
            pltpu.make_async_copy(src.at[at], dst.at[at], load_sem.at[k, i])
            for k, (src, dst) in enumerate(((den_hbm, den), (ket_hbm, ket), (bra_hbm, bra)))
        ]

    def start_loads(i, carry):
        for copy in loads(i):
            copy.start()
        return carry

    start_loads(0, 0)
    for copy in small:
        copy.start()

    barrier = pltpu.get_barrier_semaphore()
    for o in range(1, groups):
        g = lax.rem(me + o, groups)
        pl.semaphore_signal(
            barrier, inc=1, device_id=(g // nz, lax.rem(g, nz) * 2 + core), device_id_type=MESH
        )
    for k in range(nz):
        pl.semaphore_signal(barrier, inc=1, device_id=(s, k * 2 + 1 - core), device_id_type=MESH)

    lax.fori_loop(1, chunks, start_loads, 0)
    u_copy = pltpu.make_async_copy(u_hbm, u_ref, table_sem.at[0])
    u_copy.start()
    piece = n_types // PIECES
    t_copies = []
    for i in range(PIECES):
        at = pl.ds(i * piece, piece)
        t_copies.append(pltpu.make_async_copy(t_hbm.at[at], t_ref.at[at], table_sem.at[1 + i]))
        t_copies[i].start()

    def moments(i, carry):
        for copy in loads(i):
            copy.wait()
        rows = []
        for u in range(GROUP):
            b = i * GROUP + u
            inner = dot(den[b], ket[b], NN)
            rows.append(jnp.sum(inner * bra[b].astype(F32), axis=0, keepdims=True))
        mom[pl.ds(i * GROUP, GROUP), :] = jnp.concatenate(rows, axis=0)
        return carry

    early = chunks // 3
    turns = max(n for n in range(1, chunks - early + 1) if (groups - 1) % n == 0)
    each = (groups - 1) // turns
    lax.fori_loop(0, early, moments, 0)

    for copy in small:
        copy.wait()
    lists[pl.ds(me * 16, 8), 0:entries] = ltype_ref[...] * KEY + lsrc_ref[...]
    lists[pl.ds(me * 16 + 8, 1), 0:entries] = ctype_ref[...] * KEY + csrc_ref[...]
    pl.semaphore_wait(barrier, groups - 1 + nz)

    def list_copy(o):
        g = lax.rem(me + o, groups)
        at = pl.ds(me * 16, 16)
        return pltpu.make_async_remote_copy(
            src_ref=lists.at[at],
            dst_ref=lists.at[at],
            send_sem=list_send.at[o],
            recv_sem=list_recv.at[me],
            device_id=(g // nz, lax.rem(g, nz) * 2 + core),
            device_id_type=MESH,
        )

    def list_arrival(o):
        g = lax.rem(me + o, groups)
        at = pl.ds(g * 16, 16)
        return pltpu.make_async_remote_copy(
            src_ref=lists.at[at],
            dst_ref=lists.at[at],
            send_sem=list_send.at[o],
            recv_sem=list_recv.at[g],
            device_id=(g // nz, lax.rem(g, nz) * 2 + core),
            device_id_type=MESH,
        )

    def moments_and_lists(i, carry):
        for k in range(each):
            list_copy(1 + (i - early) * each + k).start()
        return moments(i, carry)

    lax.fori_loop(early, early + turns, moments_and_lists, 0)
    lax.fori_loop(early + turns, chunks, moments, 0)
    hot = jnp.where(
        lax.broadcasted_iota(jnp.int32, (box_dom, n_blocks), 0) == box_ref[...], 1.0, 0.0
    ).astype(BF16)
    part[...] = one_hot_dot(hot, mom[...], NN)

    sib_copy = pltpu.make_async_remote_copy(
        src_ref=part,
        dst_ref=sib,
        send_sem=sib_send,
        recv_sem=sib_recv,
        device_id=(s, other),
        device_id_type=MESH,
    )
    sib_copy.start()
    same = lax.broadcasted_iota(jnp.int32, (box_dom, box_dom), 0) == lax.broadcasted_iota(
        jnp.int32, (box_dom, box_dom), 1
    )
    hot_rows[...] = dot(hot, jnp.where(same, 1.0, 0.0).astype(BF16), TN)

    for o in range(1, groups):
        list_arrival(o).wait_recv()
    for w in range(3):
        sender_at = 2 - w
        target = jnp.clip(s + w - 1, 0, n_space - 1)
        for k in range(nz):
            packed = lists[pl.ds((target * nz + k) * 16, 8), 0:entries]
            kind = lax.shift_right_logical(packed, 10)
            place = (packed & (KEY - 1)) - sender_at * box_dom
            keys = jnp.where((place >= 0) & (place < box_dom), kind * box_dom + place, -1)
            c_leaf[pl.ds((w * nz + k) * 8, 8), :] = count_hot(keys, n_types * box_dom)
    packed = lists[pl.ds(8, groups, stride=16), :]
    kind = lax.shift_right_logical(packed, 10)
    place = (packed & (KEY - 1)) - s * top_dom
    keys = jnp.where((place >= 0) & (place < top_dom), kind * top_dom + place, -1)
    c_top[...] = count_hot(keys[:, 0:entries], n_types * top_dom)

    u_copy.wait()
    sib_copy.wait()
    own = part[...] + sib[...]
    x_ref[0:box_dom, :] = own
    kids[0:box_dom, :] = own[:, 0:128]
    kids[box_dom:, :] = own[:, 128:]
    x_ref[box_dom:, :] = jnp.zeros((x_ref.shape[0] - box_dom, x_ref.shape[1]), F32)

    tops = jnp.zeros((top_dom, x_ref.shape[1]), F32)
    for c in range(8):
        child = jnp.concatenate(
            [kids[pl.ds(h * box_dom + c, top_dom, stride=8), :] for h in range(2)], axis=1
        )
        c_high, c_low = halves(child)
        stack = jnp.concatenate([c_high.astype(F32), c_low.astype(F32)], axis=0).astype(BF16)
        u_high, u_low = halves(u_ref[c])
        both = dot(stack, u_high, NT)
        extra = dot(stack, u_low, NT)
        tops += both[:top_dom] + both[top_dom:] + extra[:top_dom]
    x_ref[box_dom : box_dom + top_dom, :] = tops

    x = x_ref[...]
    x_high, x_low = halves(x)
    x_rows = x.shape[0]
    stack = jnp.concatenate([x_high, x_low], axis=0)
    for t in range(n_types):
        if t % piece == 0:
            t_copies[t // piece].wait()
        t_high, t_low = halves(t_ref[t])
        both = dot(stack, t_high, NT)
        v = both[:x_rows] + both[x_rows:] + dot(x_high, t_low, NT)
        high, low = halves(v[:box_dom])
        v_high[t * box_dom : (t + 1) * box_dom, :] = high
        v_low[t * box_dom : (t + 1) * box_dom, :] = low
        v_top[t * top_dom : (t + 1) * top_dom, :] = v[box_dom : box_dom + top_dom]

    sent_top = one_hot_dot(c_top[...].astype(BF16), v_top[...], NN)
    for g in range(groups):
        top_out[g] = sent_top[g : g + 1, :]

    def top_copy(o, source):
        g = lax.rem(me + o, groups)
        return pltpu.make_async_remote_copy(
            src_ref=top_out.at[g],
            dst_ref=top_in.at[source],
            send_sem=top_send.at[o],
            recv_sem=top_recv.at[source],
            device_id=(g // nz, lax.rem(g, nz) * 2 + core),
            device_id_type=MESH,
        )

    for o in range(1, groups):
        top_copy(o, me).start()
    top_in[pl.ds(me, 1)] = top_out[pl.ds(me, 1)]

    hot_leaf = c_leaf[...].astype(BF16)
    sent = dot(hot_leaf, v_high[...], NN) + dot(hot_leaf, v_low[...], NN)
    leaf_out[...] = sent.reshape(3 * nz, 8, sent.shape[1])

    def leaf_copy(w, o, source):
        k = lax.rem(z + o, nz)
        n = w * nz + o
        return pltpu.make_async_remote_copy(
            src_ref=leaf_out.at[w * nz + k],
            dst_ref=leaf_in.at[source],
            send_sem=leaf_send.at[n],
            recv_sem=leaf_recv.at[source],
            device_id=(jnp.clip(s + w - 1, 0, n_space - 1), k * 2 + core),
            device_id_type=MESH,
        )

    has = (s > 0, None, s < n_space - 1)
    for w in (0, 2):
        @pl.when(has[w])
        def _():
            for o in range(nz):
                leaf_copy(w, o, (2 - w) * nz + z).start()
    for o in range(1, nz):
        leaf_copy(1, o, nz + z).start()

    total = jnp.zeros((1, x_ref.shape[1]), F32)
    for o in range(1, groups):
        top_copy(o, lax.rem(me + o, groups)).wait_recv()
    for g in range(groups):
        total += top_in[g]
    total_high, total_low = halves(total)
    stack = jnp.concatenate(
        [total_high.astype(F32), total_low.astype(F32), jnp.zeros((14, total.shape[1]), F32)], axis=0
    ).astype(BF16)
    down = []
    for c in range(8):
        u_high, u_low = halves(u_ref[c])
        both = dot(stack, u_high, NN)
        extra = dot(stack, u_low, NN)
        down.append(both[0:1] + both[1:2] + extra[0:1])
    acc[...] = jnp.concatenate(down, axis=0) + leaf_out[pl.ds(nz + z, 1)][0]
    for o in range(1, nz):
        source = nz + lax.rem(z + o, nz)
        leaf_copy(1, o, source).wait_recv()
        acc[...] += leaf_in[pl.ds(source, 1)][0]
    for w in (0, 2):
        @pl.when(has[w])
        def _():
            for o in range(nz):
                source = w * nz + lax.rem(z + o, nz)
                leaf_copy(w, o, source).wait_recv()
                acc[...] += leaf_in[pl.ds(source, 1)][0]
    mine_ref[...] = acc[...]
    here = pl.ds(j * 8, 8)
    dom[here, :] = acc[...]

    def dom_copy(o, source):
        at = pl.ds(source * 8, 8)
        return pltpu.make_async_remote_copy(
            src_ref=dom.at[at],
            dst_ref=dom.at[at],
            send_sem=dom_send.at[o],
            recv_sem=dom_recv.at[source],
            device_id=(s, lax.rem(j + o, n_blk)),
            device_id_type=MESH,
        )

    for o in range(1, n_blk):
        dom_copy(o, j).start()

    for o in range(1, groups):
        list_copy(o).wait_send()
        top_copy(o, me).wait_send()
    for w in (0, 2):
        @pl.when(has[w])
        def _():
            for o in range(nz):
                leaf_copy(w, o, (2 - w) * nz + z).wait_send()
    for o in range(1, nz):
        leaf_copy(1, o, nz + z).wait_send()

    for o in range(1, n_blk):
        dom_copy(o, lax.rem(j + o, n_blk)).wait_recv()
    rows_ref[...] = one_hot_dot(hot_rows[...].astype(BF16), dom[...], NN)
    for o in range(1, n_blk):
        dom_copy(o, j).wait_send()


def contract(bra, ket, rows_ref, mine_ref, out_hbm, mine_hbm, out, out_sem, mine_sem):
    mine_copy = pltpu.make_async_copy(mine_ref, mine_hbm, mine_sem)
    mine_copy.start()

    def store(i):
        at = pl.ds(i * STEP, STEP)
        return pltpu.make_async_copy(out.at[at], out_hbm.at[at], out_sem.at[i])

    def step(i, carry):
        local = rows_ref[pl.ds(i * STEP, STEP), :]
        for first in range(0, STEP, 4):
            made = []
            for u in range(first, first + 4):
                b = i * STEP + u
                scaled = (bra[b].astype(F32) * local[u : u + 1, :]).astype(BF16)
                made.append(dot(scaled, ket[b], NT).astype(BF16))
            for u in range(4):
                out[i * STEP + first + u] = made[u]
        store(i).start()
        return carry

    steps = bra.shape[0] // STEP
    lax.fori_loop(0, steps, step, 0)
    for i in range(steps):
        store(i).wait()
    mine_copy.wait()


def shards(
    density,
    bra_table,
    ket_table,
    box_of_block,
    leaf_src,
    leaf_type,
    coarse_src,
    coarse_type,
    translation,
    upward_translation_table,
):
    n_space = lax.axis_size("space")
    n_blk = lax.axis_size("blk")
    nz = n_blk // 2
    groups = n_space * nz
    n_blocks, side, coeffs = bra_table.shape
    n_types = translation.shape[0]
    box_dom = 8 * n_blk
    top_dom = n_blk
    chunks = n_blocks // GROUP
    x_rows = -(-(box_dom + top_dom) // 16) * 16
    whole = pl.BlockSpec(memory_space=pltpu.VMEM)
    far = pl.BlockSpec(memory_space=pltpu.HBM)
    dma = pltpu.SemaphoreType.DMA
    ints = jnp.int32
    bra_here, ket_here, rows, mine = pl.pallas_call(
        functools.partial(build, n_space, n_blk, n_types),
        out_shape=(
            jax.ShapeDtypeStruct(bra_table.shape, BF16),
            jax.ShapeDtypeStruct(ket_table.shape, BF16),
            jax.ShapeDtypeStruct((n_blocks, coeffs), F32),
            jax.ShapeDtypeStruct((8, coeffs), F32),
        ),
        in_specs=[far] * 10,
        out_specs=(whole,) * 4,
        scratch_shapes=[
            pltpu.VMEM((1, n_blocks), ints),
            pltpu.VMEM(leaf_src.shape, ints),
            pltpu.VMEM(leaf_type.shape, ints),
            pltpu.VMEM(coarse_src.shape, ints),
            pltpu.VMEM(coarse_type.shape, ints),
            pltpu.VMEM(density.shape, BF16),
            pltpu.VMEM(translation.shape, F32),
            pltpu.VMEM(upward_translation_table.shape, F32),
            pltpu.VMEM((n_blocks, coeffs), F32),
            pltpu.VMEM((box_dom, coeffs), F32),
            pltpu.VMEM((box_dom, coeffs), F32),
            pltpu.VMEM((groups * 16, 128), jnp.int32),
            pltpu.VMEM((3 * nz * 8, n_types * box_dom), F32),
            pltpu.VMEM((groups, n_types * top_dom), F32),
            pltpu.VMEM((x_rows, coeffs), F32),
            pltpu.VMEM((n_types * box_dom, coeffs), BF16),
            pltpu.VMEM((n_types * box_dom, coeffs), BF16),
            pltpu.VMEM((n_types * top_dom, coeffs), F32),
            pltpu.VMEM((3 * nz, 8, coeffs), F32),
            pltpu.VMEM((groups, 1, coeffs), F32),
            pltpu.VMEM((3 * nz, 8, coeffs), F32),
            pltpu.VMEM((groups, 1, coeffs), F32),
            pltpu.VMEM((box_dom, coeffs), F32),
            pltpu.VMEM((8, coeffs), F32),
            pltpu.VMEM((2 * box_dom, coeffs // 2), F32),
            pltpu.VMEM((n_blocks, box_dom), F32),
            dma((5,)),
            dma((3, chunks)),
            dma((1 + PIECES,)),
            dma((groups,)),
            dma((groups,)),
            dma,
            dma,
            dma((3 * nz,)),
            dma((3 * nz,)),
            dma((groups,)),
            dma((groups,)),
            dma((n_blk,)),
            dma((n_blk,)),
        ],
        compiler_params=pltpu.CompilerParams(
            collective_id=0, has_side_effects=True, vmem_limit_bytes=28 * 1024 * 1024
        ),
        cost_estimate=pl.CostEstimate(
            flops=2 * n_blocks * side * side * coeffs,
            bytes_accessed=22_000_000,
            transcendentals=0,
        ),
    )(
        *(
            pltpu.with_memory_space_constraint(x, pltpu.HBM)
            for x in (
                density,
                bra_table,
                ket_table,
                box_of_block[None, :],
                leaf_src,
                leaf_type,
                coarse_src,
                coarse_type,
                translation,
                upward_translation_table,
            )
        )
    )
    return pl.pallas_call(
        contract,
        out_shape=(
            jax.ShapeDtypeStruct((n_blocks, side, side), BF16),
            jax.ShapeDtypeStruct((8, coeffs), F32),
        ),
        in_specs=[whole] * 4,
        out_specs=(far, far),
        scratch_shapes=[
            pltpu.VMEM((n_blocks, side, side), BF16),
            dma((n_blocks // STEP,)),
            dma,
        ],
        compiler_params=pltpu.CompilerParams(vmem_limit_bytes=16 * 1024 * 1024),
        cost_estimate=pl.CostEstimate(
            flops=2 * n_blocks * side * side * coeffs,
            bytes_accessed=2 * n_blocks * side * side,
            transcendentals=0,
        ),
    )(bra_here, ket_here, rows, mine)


def solution(mesh):
    placed = (
        P(("space", "blk"), None, None),
        P(("space", "blk"), None, None),
        P(("space", "blk"), None, None),
        P(("space", "blk")),
        P(("space", "blk"), None),
        P(("space", "blk"), None),
        P(("space", "blk"), None),
        P(("space", "blk"), None),
        P(),
        P(),
    )
    return jax.shard_map(
        shards,
        mesh=mesh,
        in_specs=placed,
        out_specs=(P(("space", "blk"), None, None), P(("space", "blk"), None)),
        check_vma=False,
    )
```

```python
import functools

import jax
import jax.numpy as jnp
from jax import lax
from jax.experimental import pallas as pl
from jax.experimental.pallas import tpu as pltpu
from jax.sharding import PartitionSpec as P

MESH = pl.DeviceIdType.MESH
F32 = jnp.float32
BF16 = jnp.bfloat16
GROUP = 16
STEP = 16
PIECES = 4
KEY = 1024


def dot(a, b, dims):
    return lax.dot_general(a, b, (dims, ((), ())), preferred_element_type=F32)


NN = ((1,), (0,))
NT = ((1,), (1,))
TN = ((0,), (0,))


def halves(x):
    high = x.astype(BF16)
    return high, (x - high.astype(F32)).astype(BF16)


def one_hot_dot(hot, x, dims):
    high, low = halves(x)
    return dot(hot, high, dims) + dot(hot, low, dims)


def count_hot(keys, width):
    rows, entries = keys.shape
    lane = lax.broadcasted_iota(jnp.int32, (rows, width), 1)
    total = jnp.zeros((rows, width), F32)
    for e in range(entries):
        total += jnp.where(lane == keys[:, e : e + 1], 1.0, 0.0)
    return total


def build(
    n_space,
    n_blk,
    n_types,
    den_hbm, bra_hbm, ket_hbm, box_hbm, lsrc_hbm, ltype_hbm, csrc_hbm, ctype_hbm, t_hbm, u_hbm,
    bra, ket, rows_ref, mine_ref,
    box_ref, lsrc_ref, ltype_ref, csrc_ref, ctype_ref, den, t_ref, u_ref, mom, part, sib, lists, c_leaf, c_top, x_ref, v_high, v_low, v_top,
    leaf_out, top_out, leaf_in, top_in, dom, acc, kids, hot_rows,
    small_sem, load_sem, table_sem, list_send, list_recv, sib_send, sib_recv,
    leaf_send, leaf_recv, top_send, top_recv, dom_send, dom_recv,
):
    s = lax.axis_index("space")
    j = lax.axis_index("blk")
    core = lax.rem(j, 2)
    z = j // 2
    other = j + 1 - 2 * core
    nz = n_blk // 2
    box_dom = 8 * n_blk
    top_dom = n_blk
    n_blocks = den.shape[0]
    chunks = n_blocks // GROUP
    entries = lsrc_ref.shape[1]
    me = s * nz + z
    groups = n_space * nz

    small = [
        pltpu.make_async_copy(src, dst, small_sem.at[k])
        for k, (src, dst) in enumerate(
            (
                (ltype_hbm, ltype_ref),
                (lsrc_hbm, lsrc_ref),
                (ctype_hbm, ctype_ref),
                (csrc_hbm, csrc_ref),
                (box_hbm, box_ref),
            )
        )
    ]

    def loads(i):
        at = pl.ds(i * GROUP, GROUP)
        return [
            pltpu.make_async_copy(src.at[at], dst.at[at], load_sem.at[k, i])
            for k, (src, dst) in enumerate(((den_hbm, den), (ket_hbm, ket), (bra_hbm, bra)))
        ]

    def start_loads(i, carry):
        for copy in loads(i):
            copy.start()
        return carry

    start_loads(0, 0)
    for copy in small:
        copy.start()

    barrier = pltpu.get_barrier_semaphore()
    for o in range(1, groups):
        g = lax.rem(me + o, groups)
        pl.semaphore_signal(
            barrier, inc=1, device_id=(g // nz, lax.rem(g, nz) * 2 + core), device_id_type=MESH
        )
    for k in range(nz):
        pl.semaphore_signal(barrier, inc=1, device_id=(s, k * 2 + 1 - core), device_id_type=MESH)

    lax.fori_loop(1, chunks, start_loads, 0)
    u_copy = pltpu.make_async_copy(u_hbm, u_ref, table_sem.at[0])
    u_copy.start()
    piece = n_types // PIECES
    t_copies = []
    for i in range(PIECES):
        at = pl.ds(i * piece, piece)
        t_copies.append(pltpu.make_async_copy(t_hbm.at[at], t_ref.at[at], table_sem.at[1 + i]))
        t_copies[i].start()

    def moments(i, carry):
        for copy in loads(i):
            copy.wait()
        rows = []
        for u in range(GROUP):
            b = i * GROUP + u
            inner = dot(den[b], ket[b], NN)
            rows.append(jnp.sum(inner * bra[b].astype(F32), axis=0, keepdims=True))
        mom[pl.ds(i * GROUP, GROUP), :] = jnp.concatenate(rows, axis=0)
        return carry

    early = chunks // 3
    turns = max(n for n in range(1, chunks - early + 1) if (groups - 1) % n == 0)
    each = (groups - 1) // turns
    lax.fori_loop(0, early, moments, 0)

    for copy in small:
        copy.wait()
    lists[pl.ds(me * 16, 8), 0:entries] = ltype_ref[...] * KEY + lsrc_ref[...]
    lists[pl.ds(me * 16 + 8, 1), 0:entries] = ctype_ref[...] * KEY + csrc_ref[...]
    pl.semaphore_wait(barrier, groups - 1 + nz)

    def list_copy(o):
        g = lax.rem(me + o, groups)
        at = pl.ds(me * 16, 16)
        return pltpu.make_async_remote_copy(
            src_ref=lists.at[at],
            dst_ref=lists.at[at],
            send_sem=list_send.at[o],
            recv_sem=list_recv.at[me],
            device_id=(g // nz, lax.rem(g, nz) * 2 + core),
            device_id_type=MESH,
        )

    def list_arrival(o):
        g = lax.rem(me + o, groups)
        at = pl.ds(g * 16, 16)
        return pltpu.make_async_remote_copy(
            src_ref=lists.at[at],
            dst_ref=lists.at[at],
            send_sem=list_send.at[o],
            recv_sem=list_recv.at[g],
            device_id=(g // nz, lax.rem(g, nz) * 2 + core),
            device_id_type=MESH,
        )

    def moments_and_lists(i, carry):
        for k in range(each):
            list_copy(1 + (i - early) * each + k).start()
        return moments(i, carry)

    lax.fori_loop(early, early + turns, moments_and_lists, 0)
    lax.fori_loop(early + turns, chunks, moments, 0)
    hot = jnp.where(
        lax.broadcasted_iota(jnp.int32, (box_dom, n_blocks), 0) == box_ref[...], 1.0, 0.0
    ).astype(BF16)
    part[...] = one_hot_dot(hot, mom[...], NN)

    sib_copy = pltpu.make_async_remote_copy(
        src_ref=part,
        dst_ref=sib,
        send_sem=sib_send,
        recv_sem=sib_recv,
        device_id=(s, other),
        device_id_type=MESH,
    )
    sib_copy.start()
    same = lax.broadcasted_iota(jnp.int32, (box_dom, box_dom), 0) == lax.broadcasted_iota(
        jnp.int32, (box_dom, box_dom), 1
    )
    hot_rows[...] = dot(hot, jnp.where(same, 1.0, 0.0).astype(BF16), TN)

    for o in range(1, groups):
        list_arrival(o).wait_recv()
    for w in range(3):
        sender_at = 2 - w
        target = jnp.clip(s + w - 1, 0, n_space - 1)
        for k in range(nz):
            packed = lists[pl.ds((target * nz + k) * 16, 8), 0:entries]
            kind = lax.shift_right_logical(packed, 10)
            place = (packed & (KEY - 1)) - sender_at * box_dom
            keys = jnp.where((place >= 0) & (place < box_dom), kind * box_dom + place, -1)
            c_leaf[pl.ds((w * nz + k) * 8, 8), :] = count_hot(keys, n_types * box_dom)
    packed = lists[pl.ds(8, groups, stride=16), :]
    kind = lax.shift_right_logical(packed, 10)
    place = (packed & (KEY - 1)) - s * top_dom
    keys = jnp.where((place >= 0) & (place < top_dom), kind * top_dom + place, -1)
    c_top[...] = count_hot(keys[:, 0:entries], n_types * top_dom)

    u_copy.wait()
    sib_copy.wait()
    own = part[...] + sib[...]
    x_ref[0:box_dom, :] = own
    kids[0:box_dom, :] = own[:, 0:128]
    kids[box_dom:, :] = own[:, 128:]
    x_ref[box_dom:, :] = jnp.zeros((x_ref.shape[0] - box_dom, x_ref.shape[1]), F32)

    tops = jnp.zeros((top_dom, x_ref.shape[1]), F32)
    for c in range(8):
        child = jnp.concatenate(
            [kids[pl.ds(h * box_dom + c, top_dom, stride=8), :] for h in range(2)], axis=1
        )
        c_high, c_low = halves(child)
        stack = jnp.concatenate([c_high.astype(F32), c_low.astype(F32)], axis=0).astype(BF16)
        u_high, u_low = halves(u_ref[c])
        both = dot(stack, u_high, NT)
        extra = dot(stack, u_low, NT)
        tops += both[:top_dom] + both[top_dom:] + extra[:top_dom]
    x_ref[box_dom : box_dom + top_dom, :] = tops

    x = x_ref[...]
    x_high, x_low = halves(x)
    x_rows = x.shape[0]
    stack = jnp.concatenate([x_high, x_low], axis=0)
    for t in range(n_types):
        if t % piece == 0:
            t_copies[t // piece].wait()
        t_high, t_low = halves(t_ref[t])
        both = dot(stack, t_high, NT)
        v = both[:x_rows] + both[x_rows:] + dot(x_high, t_low, NT)
        high, low = halves(v[:box_dom])
        v_high[t * box_dom : (t + 1) * box_dom, :] = high
        v_low[t * box_dom : (t + 1) * box_dom, :] = low
        v_top[t * top_dom : (t + 1) * top_dom, :] = v[box_dom : box_dom + top_dom]

    sent_top = one_hot_dot(c_top[...].astype(BF16), v_top[...], NN)
    for g in range(groups):
        top_out[g] = sent_top[g : g + 1, :]

    def top_copy(o, source):
        g = lax.rem(me + o, groups)
        return pltpu.make_async_remote_copy(
            src_ref=top_out.at[g],
            dst_ref=top_in.at[source],
            send_sem=top_send.at[o],
            recv_sem=top_recv.at[source],
            device_id=(g // nz, lax.rem(g, nz) * 2 + core),
            device_id_type=MESH,
        )

    for o in range(1, groups):
        top_copy(o, me).start()
    top_in[pl.ds(me, 1)] = top_out[pl.ds(me, 1)]

    hot_leaf = c_leaf[...].astype(BF16)
    sent = dot(hot_leaf, v_high[...], NN) + dot(hot_leaf, v_low[...], NN)
    leaf_out[...] = sent.reshape(3 * nz, 8, sent.shape[1])

    def leaf_copy(w, o, source):
        k = lax.rem(z + o, nz)
        n = w * nz + o
        return pltpu.make_async_remote_copy(
            src_ref=leaf_out.at[w * nz + k],
            dst_ref=leaf_in.at[source],
            send_sem=leaf_send.at[n],
            recv_sem=leaf_recv.at[source],
            device_id=(jnp.clip(s + w - 1, 0, n_space - 1), k * 2 + core),
            device_id_type=MESH,
        )

    has = (s > 0, None, s < n_space - 1)
    for w in (0, 2):
        @pl.when(has[w])
        def _():
            for o in range(nz):
                leaf_copy(w, o, (2 - w) * nz + z).start()
    for o in range(1, nz):
        leaf_copy(1, o, nz + z).start()

    total = jnp.zeros((1, x_ref.shape[1]), F32)
    for o in range(1, groups):
        top_copy(o, lax.rem(me + o, groups)).wait_recv()
    for g in range(groups):
        total += top_in[g]
    total_high, total_low = halves(total)
    stack = jnp.concatenate(
        [total_high.astype(F32), total_low.astype(F32), jnp.zeros((14, total.shape[1]), F32)], axis=0
    ).astype(BF16)
    down = []
    for c in range(8):
        u_high, u_low = halves(u_ref[c])
        both = dot(stack, u_high, NN)
        extra = dot(stack, u_low, NN)
        down.append(both[0:1] + both[1:2] + extra[0:1])
    acc[...] = jnp.concatenate(down, axis=0) + leaf_out[pl.ds(nz + z, 1)][0]
    for o in range(1, nz):
        source = nz + lax.rem(z + o, nz)
        leaf_copy(1, o, source).wait_recv()
        acc[...] += leaf_in[pl.ds(source, 1)][0]
    for w in (0, 2):
        @pl.when(has[w])
        def _():
            for o in range(nz):
                source = w * nz + lax.rem(z + o, nz)
                leaf_copy(w, o, source).wait_recv()
                acc[...] += leaf_in[pl.ds(source, 1)][0]
    mine_ref[...] = acc[...]
    here = pl.ds(j * 8, 8)
    dom[here, :] = acc[...]

    def dom_copy(o, source):
        at = pl.ds(source * 8, 8)
        return pltpu.make_async_remote_copy(
            src_ref=dom.at[at],
            dst_ref=dom.at[at],
            send_sem=dom_send.at[o],
            recv_sem=dom_recv.at[source],
            device_id=(s, lax.rem(j + o, n_blk)),
            device_id_type=MESH,
        )

    for o in range(1, n_blk):
        dom_copy(o, j).start()

    for o in range(1, groups):
        list_copy(o).wait_send()
        top_copy(o, me).wait_send()
    for w in (0, 2):
        @pl.when(has[w])
        def _():
            for o in range(nz):
                leaf_copy(w, o, (2 - w) * nz + z).wait_send()
    for o in range(1, nz):
        leaf_copy(1, o, nz + z).wait_send()

    for o in range(1, n_blk):
        dom_copy(o, lax.rem(j + o, n_blk)).wait_recv()
    rows_ref[...] = one_hot_dot(hot_rows[...].astype(BF16), dom[...], NN)
    for o in range(1, n_blk):
        dom_copy(o, j).wait_send()


def contract(bra, ket, rows_ref, mine_ref, out_hbm, mine_hbm, out, out_sem, mine_sem):
    mine_copy = pltpu.make_async_copy(mine_ref, mine_hbm, mine_sem)
    mine_copy.start()

    def store(i):
        at = pl.ds(i * STEP, STEP)
        return pltpu.make_async_copy(out.at[at], out_hbm.at[at], out_sem.at[i])

    def step(i, carry):
        local = rows_ref[pl.ds(i * STEP, STEP), :]
        for first in range(0, STEP, 4):
            made = []
            for u in range(first, first + 4):
                b = i * STEP + u
                scaled = (bra[b].astype(F32) * local[u : u + 1, :]).astype(BF16)
                made.append(dot(scaled, ket[b], NT).astype(BF16))
            for u in range(4):
                out[i * STEP + first + u] = made[u]
        store(i).start()
        return carry

    steps = bra.shape[0] // STEP
    lax.fori_loop(0, steps, step, 0)
    for i in range(steps):
        store(i).wait()
    mine_copy.wait()


def shards(
    density,
    bra_table,
    ket_table,
    box_of_block,
    leaf_src,
    leaf_type,
    coarse_src,
    coarse_type,
    translation,
    upward_translation_table,
):
    n_space = lax.axis_size("space")
    n_blk = lax.axis_size("blk")
    nz = n_blk // 2
    groups = n_space * nz
    n_blocks, side, coeffs = bra_table.shape
    n_types = translation.shape[0]
    box_dom = 8 * n_blk
    top_dom = n_blk
    chunks = n_blocks // GROUP
    x_rows = -(-(box_dom + top_dom) // 16) * 16
    whole = pl.BlockSpec(memory_space=pltpu.VMEM)
    far = pl.BlockSpec(memory_space=pltpu.HBM)
    dma = pltpu.SemaphoreType.DMA
    ints = jnp.int32
    bra_here, ket_here, rows, mine = pl.pallas_call(
        functools.partial(build, n_space, n_blk, n_types),
        out_shape=(
            jax.ShapeDtypeStruct(bra_table.shape, BF16),
            jax.ShapeDtypeStruct(ket_table.shape, BF16),
            jax.ShapeDtypeStruct((n_blocks, coeffs), F32),
            jax.ShapeDtypeStruct((8, coeffs), F32),
        ),
        in_specs=[far] * 10,
        out_specs=(whole,) * 4,
        scratch_shapes=[
            pltpu.VMEM((1, n_blocks), ints),
            pltpu.VMEM(leaf_src.shape, ints),
            pltpu.VMEM(leaf_type.shape, ints),
            pltpu.VMEM(coarse_src.shape, ints),
            pltpu.VMEM(coarse_type.shape, ints),
            pltpu.VMEM(density.shape, BF16),
            pltpu.VMEM(translation.shape, F32),
            pltpu.VMEM(upward_translation_table.shape, F32),
            pltpu.VMEM((n_blocks, coeffs), F32),
            pltpu.VMEM((box_dom, coeffs), F32),
            pltpu.VMEM((box_dom, coeffs), F32),
            pltpu.VMEM((groups * 16, 128), jnp.int32),
            pltpu.VMEM((3 * nz * 8, n_types * box_dom), F32),
            pltpu.VMEM((groups, n_types * top_dom), F32),
            pltpu.VMEM((x_rows, coeffs), F32),
            pltpu.VMEM((n_types * box_dom, coeffs), BF16),
            pltpu.VMEM((n_types * box_dom, coeffs), BF16),
            pltpu.VMEM((n_types * top_dom, coeffs), F32),
            pltpu.VMEM((3 * nz, 8, coeffs), F32),
            pltpu.VMEM((groups, 1, coeffs), F32),
            pltpu.VMEM((3 * nz, 8, coeffs), F32),
            pltpu.VMEM((groups, 1, coeffs), F32),
            pltpu.VMEM((box_dom, coeffs), F32),
            pltpu.VMEM((8, coeffs), F32),
            pltpu.VMEM((2 * box_dom, coeffs // 2), F32),
            pltpu.VMEM((n_blocks, box_dom), F32),
            dma((5,)),
            dma((3, chunks)),
            dma((1 + PIECES,)),
            dma((groups,)),
            dma((groups,)),
            dma,
            dma,
            dma((3 * nz,)),
            dma((3 * nz,)),
            dma((groups,)),
            dma((groups,)),
            dma((n_blk,)),
            dma((n_blk,)),
        ],
        compiler_params=pltpu.CompilerParams(
            collective_id=0, has_side_effects=True, vmem_limit_bytes=28 * 1024 * 1024
        ),
        cost_estimate=pl.CostEstimate(
            flops=2 * n_blocks * side * side * coeffs,
            bytes_accessed=22_000_000,
            transcendentals=0,
        ),
    )(
        *(
            pltpu.with_memory_space_constraint(x, pltpu.HBM)
            for x in (
                density,
                bra_table,
                ket_table,
                box_of_block[None, :],
                leaf_src,
                leaf_type,
                coarse_src,
                coarse_type,
                translation,
                upward_translation_table,
            )
        )
    )
    return pl.pallas_call(
        contract,
        out_shape=(
            jax.ShapeDtypeStruct((n_blocks, side, side), BF16),
            jax.ShapeDtypeStruct((8, coeffs), F32),
        ),
        in_specs=[whole] * 4,
        out_specs=(far, far),
        scratch_shapes=[
            pltpu.VMEM((n_blocks, side, side), BF16),
            dma((n_blocks // STEP,)),
            dma,
        ],
        compiler_params=pltpu.CompilerParams(vmem_limit_bytes=16 * 1024 * 1024),
        cost_estimate=pl.CostEstimate(
            flops=2 * n_blocks * side * side * coeffs,
            bytes_accessed=2 * n_blocks * side * side,
            transcendentals=0,
        ),
    )(bra_here, ket_here, rows, mine)


def solution(mesh):
    placed = (
        P(("space", "blk"), None, None),
        P(("space", "blk"), None, None),
        P(("space", "blk"), None, None),
        P(("space", "blk")),
        P(("space", "blk"), None),
        P(("space", "blk"), None),
        P(("space", "blk"), None),
        P(("space", "blk"), None),
        P(),
        P(),
    )
    return jax.shard_map(
        shards,
        mesh=mesh,
        in_specs=placed,
        out_specs=(P(("space", "blk"), None, None), P(("space", "blk"), None)),
        check_vma=False,
    )
```
